512 devices in a mesh: depth: 32 (over z, x_hi, core), tile: 16 (over x_lo, y).
Axes of the slice: x: 4 (x_hi: 2, x_lo: 2; x = x_hi * 2 + x_lo), y: 8, z: 8, core: 2. Of those that a mesh axis runs over, the one named last changes fastest.
Arguments:
- potential: float32 [32, 4096, 384], P('depth', 'tile'), may hold values from 0 to 3
- probe: bfloat16 [2, 256, 256], replicated, may hold values from -6 to 6
- positions: int32 [16, 67, 2], P('tile'), may hold values from 0 to 128
- intensity: bfloat16 [16, 4, 256, 256], P('tile'), may hold values from 0.099609375 to 3
- fwd_wave: float32 [32, 16, 2, 256, 256], P('depth', 'tile'), may hold values from -6 to 6
- adj_wave: bfloat16 [32, 16, 2, 256, 256], P('depth', 'tile'), may hold values from -6 to 6
- saved_wave: bfloat16 [32, 16, 4, 2, 256, 256], P('depth', 'tile'), may hold values from -6 to 6
Outputs:
- fwd_next: float32 [32, 16, 2, 256, 256], P('depth', 'tile')
- adj_next: bfloat16 [32, 16, 2, 256, 256], P('depth', 'tile')
- gradient: float32 [32, 4096, 384], P('depth', 'tile')
The draws below stay inside these ranges and needn't reach their ends.
Inputs may be any that keep to these rules, and one draw needn't show every extreme that they name: `positions`: window corners keep the whole window inside the tile's extent.
All inputs are finite; a program needn't handle non-finite values.
Results may differ from the reference program's by a relative error of at most 0.04.
Values may be sent and summed in bfloat16 or wider, within the bound.
No kernel may reach another device: no remote copies, remote signals or barrier semaphores. Data moves between devices by JAX's collectives and lax.ppermute only.
A program may use at most 64 MiB of HBM per device.

```python
import math
import jax
import jax.numpy as jnp
from jax import lax

WAVE = 256
CORE = 256
MARGIN = 64
TICKS = 4
TILE = 384
SLICES = 32
WIDTH = 4096
MICRO = 67
N_DEPTH = 32
N_TILE = 16


def with_ends(drawn, own_key, low, high):
    spot = [jax.random.randint(jax.random.fold_in(own_key, axis), (), 0, length) for axis, length in enumerate(drawn.shape)]
    main_axis = drawn.shape.index(max(drawn.shape))
    next_to = spot[:main_axis] + [(spot[main_axis] + 1) % drawn.shape[main_axis]] + spot[main_axis + 1:]
    return drawn.at[tuple(spot)].set(low).at[tuple(next_to)].set(high)


def level_of(key, dims, shards, low, top_value):
    loudness = 1.0
    for dim, blocks in shards:
        draws = jax.random.uniform(jax.random.fold_in(jax.random.fold_in(key, 6), dim), (blocks,), jnp.float32, low / len(shards), top_value / len(shards))
        loudness = loudness * jnp.repeat(jnp.exp(draws), dims[dim] // blocks).reshape((-1,) + (1,) * (len(dims) - 1 - dim))
    return loudness


def noise(key, shape, scale, bound, cuts=(), kind=jnp.bfloat16):
    factor_of = level_of(key, shape, cuts, -0.22, 0.18) if cuts else 1.0
    entries = jax.random.normal(key, shape, jnp.float32) * scale * factor_of
    return jnp.minimum(jnp.maximum(entries, -bound), bound).astype(kind)


def setup_inputs(seed: int = 0) -> dict:
    key_of = jax.random.split(jax.random.key(seed), 8)
    return {
        "potential": jnp.clip(3.0 * jax.random.uniform(key_of[0], (SLICES, WIDTH, TILE), jnp.float32) ** level_of(key_of[0], (SLICES, WIDTH, TILE), ((0, 32), (1, 16)), -0.2, 0.2), 0.0, 3.0),
        "probe": noise(key_of[1], (2, WAVE, WAVE), 1.0, 6.0),
        "positions": with_ends(jax.random.randint(key_of[2], (N_TILE, MICRO, 2), 0, TILE - WAVE + 1), jax.random.fold_in(key_of[2], 1), 0, TILE - WAVE).astype(jnp.int32),
        "intensity": jnp.clip(jnp.exp(math.log(3.0) - 3.4051113 * jax.random.uniform(key_of[3], (N_TILE, TICKS, WAVE, WAVE), jnp.float32) ** level_of(key_of[3], (N_TILE, TICKS, WAVE, WAVE), ((0, 16),), -0.2, 0.2)), 0.099609375, 3.0).astype(jnp.bfloat16),
        "fwd_wave": noise(key_of[4], (SLICES, N_TILE, 2, WAVE, WAVE), 1.0, 6.0, ((0, 32), (1, 16)), jnp.float32),
        "adj_wave": noise(key_of[5], (SLICES, N_TILE, 2, WAVE, WAVE), 1.0, 6.0, ((0, 32), (1, 16))),
        "saved_wave": noise(key_of[6], (SLICES, N_TILE, TICKS, 2, WAVE, WAVE), 1.0, 6.0, ((0, 32), (1, 16))),
    }


SIGMA = 0.8
DEFOCUS = 6.0

def tables(n):
    idx = jnp.arange(n, dtype=jnp.int32)
    prod = idx[:, None] * idx[None, :] % n
    angle = prod.astype(jnp.float32) * (2.0 * math.pi / n)
    scale = 1.0 / math.sqrt(n)
    return ((jnp.cos(angle) * scale).astype(jnp.bfloat16), (jnp.sin(angle) * scale).astype(jnp.bfloat16))

def propagator(n):
    idx = jnp.arange(n, dtype=jnp.int32)
    freq = jnp.where(idx < n // 2, idx, idx - n).astype(jnp.float32)
    square = freq[:, None] * freq[:, None] + freq[None, :] * freq[None, :]
    phase = -math.pi * DEFOCUS * square / (n * n)
    return (jnp.cos(phase), jnp.sin(phase))

def to_half(value):
    return lax.optimization_barrier(value.astype(jnp.bfloat16)).astype(jnp.float32)

def product(left, right):
    return jnp.dot(left, right, precision=lax.Precision.HIGHEST)

def transform(real, imag, cos_t, sin_t, sign):
    xr = to_half(real)
    xi = to_half(imag)
    ar = product(cos_t, xr) + sign * product(sin_t, xi)
    ai = product(cos_t, xi) - sign * product(sin_t, xr)
    ar = to_half(ar)
    ai = to_half(ai)
    br = product(ar, cos_t) + sign * product(ai, sin_t)
    bi = product(ai, cos_t) - sign * product(ar, sin_t)
    return (br, bi)

def forward_section(wave, window, intens, is_last, cos_t, sin_t, prop_r, prop_i):
    trans_r = jnp.cos(SIGMA * window)
    trans_i = jnp.sin(SIGMA * window)
    ur = trans_r * wave[0] - trans_i * wave[1]
    ui = trans_r * wave[1] + trans_i * wave[0]
    big_r, big_i = transform(ur, ui, cos_t, sin_t, 1.0)
    far_r = big_r * prop_r - big_i * prop_i
    far_i = big_r * prop_i + big_i * prop_r
    excess = far_r * far_r + far_i * far_i - intens.astype(jnp.float32)
    src_r = jnp.where(is_last, excess * far_r, far_r)
    src_i = jnp.where(is_last, excess * far_i, far_i)
    out_r, out_i = transform(src_r, src_i, cos_t, sin_t, -1.0)
    return jnp.stack([out_r, out_i])

def backward_section(adjoint, saved, window, cos_t, sin_t, prop_r, prop_i):
    lr, li = transform(adjoint[0].astype(jnp.float32), adjoint[1].astype(jnp.float32), cos_t, sin_t, 1.0)
    mr = lr * prop_r + li * prop_i
    mi = li * prop_r - lr * prop_i
    lur, lui = transform(mr, mi, cos_t, sin_t, -1.0)
    trans_r = jnp.cos(SIGMA * window)
    trans_i = jnp.sin(SIGMA * window)
    saved_r = saved[0].astype(jnp.float32)
    saved_i = saved[1].astype(jnp.float32)
    uar = trans_r * saved_r - trans_i * saved_i
    uai = trans_r * saved_i + trans_i * saved_r
    delta = SIGMA * (lui * uar - lur * uai)
    back = jnp.stack([trans_r * lur + trans_i * lui, trans_r * lui - trans_i * lur])
    return (back, delta)

def reference(potential, probe, positions, intensity, fwd_wave, adj_wave, saved_wave):
    n = WAVE
    sections = N_DEPTH
    tiles = N_TILE
    core = CORE
    margin = MARGIN
    cos_h, sin_h = tables(n)
    cos_t = cos_h.astype(jnp.float32)
    sin_t = sin_h.astype(jnp.float32)
    prop_r, prop_i = propagator(n)
    padded = jnp.pad(potential, ((0, 0), (margin, margin), (0, 0)))
    section_ids = jnp.arange(sections, dtype=jnp.int32)
    last_mask = section_ids == sections - 1
    probe_wave = probe.astype(jnp.float32)

    def cut(extent, corner):
        return lax.dynamic_slice(extent, (corner[0], corner[1]), (n, n))

    def place(grad, delta, corner):
        old = lax.dynamic_slice(grad, (corner[0], corner[1]), (n, n))
        return lax.dynamic_update_slice(grad, old + delta, (corner[0], corner[1]))

    def one_tile(inputs):
        tile_index, spots, intens, wave, adjoint, saved = inputs
        start = (tile_index * core).astype(jnp.int32)
        extent = lax.dynamic_slice(padded, (jnp.int32(0), start, jnp.int32(0)), (sections, core + 2 * margin, TILE))
        grad = jnp.zeros((sections, core + 2 * margin, TILE), jnp.float32)
        for tick in range(TICKS):
            f_pos = spots[tick - section_ids + 2 * sections - 1]
            a_pos = spots[tick + section_ids]
            f_win = jax.vmap(cut)(extent, f_pos)
            a_win = jax.vmap(cut)(extent, a_pos)
            sent = jax.vmap(lambda w, v, last: forward_section(w, v, intens[tick], last, cos_t, sin_t, prop_r, prop_i))(wave, f_win, last_mask)
            back, delta = jax.vmap(lambda a, s, v: backward_section(a, s, v, cos_t, sin_t, prop_r, prop_i))(adjoint, saved[:, tick], a_win)
            grad = jax.vmap(place)(grad, delta, a_pos)
            wave = jnp.concatenate([probe_wave[None], sent[:-1]], 0)
            adjoint = jnp.concatenate([back[1:], sent[-1:]], 0).astype(jnp.bfloat16)
        return (wave, adjoint, grad)
    tile_ids = jnp.arange(tiles, dtype=jnp.int32)
    waves, adjoints, grads = lax.map(one_tile, (tile_ids, positions, intensity, jnp.swapaxes(fwd_wave, 0, 1), jnp.swapaxes(adj_wave, 0, 1), jnp.swapaxes(saved_wave, 0, 1)))
    inner = grads[:, :, margin:margin + core]
    zeros = jnp.zeros((1, sections, margin, TILE), jnp.float32)
    from_left = jnp.concatenate([zeros, grads[:-1, :, margin + core:]], 0)
    from_right = jnp.concatenate([grads[1:, :, :margin], zeros], 0)
    inner = inner + jnp.pad(from_left, ((0, 0), (0, 0), (0, core - margin), (0, 0)))
    inner = inner + jnp.pad(from_right, ((0, 0), (0, 0), (core - margin, 0), (0, 0)))
    gradient = jnp.swapaxes(inner, 0, 1).reshape(sections, tiles * core, TILE)
    return (jnp.swapaxes(waves, 0, 1), jnp.swapaxes(adjoints, 0, 1), gradient)
```

```python
import functools
import math

import jax
import jax.numpy as jnp
import numpy as np
from jax import lax
from jax.experimental import pallas as pl
from jax.experimental.pallas import tpu as pltpu
from jax.sharding import PartitionSpec as P

TICKS = 4
SIGMA = 0.8
DEFOCUS = 6.0
LANES = 128
SUB = 8
F32 = jnp.float32
BF16 = jnp.bfloat16


def dft_matrices(n):
    idx = np.arange(n)
    angle = ((idx[:, None] * idx[None, :]) % n).astype(np.float32) * np.float32(2.0 * math.pi / n)
    scale = np.float32(1.0 / math.sqrt(n))
    cos_t = np.cos(angle) * scale
    sin_t = np.sin(angle) * scale
    both = np.block([[cos_t, sin_t], [-sin_t, cos_t]])
    return both.astype(BF16), np.ascontiguousarray(both.T).astype(BF16)


def propagator(n):
    idx = np.arange(n)
    freq = np.where(idx < n // 2, idx, idx - n).astype(np.float32)
    square = freq[:, None] * freq[:, None] + freq[None, :] * freq[None, :]
    phase = np.float32(-math.pi * DEFOCUS) * square / np.float32(n * n)
    return np.cos(phase).astype(np.float32), np.sin(phase).astype(np.float32)


def sin_cos(x):
    mid = 1.2
    y = x - mid
    z = y * y
    s = y * (1.0 + z * (-1.0 / 6 + z * (1.0 / 120 + z * (-1.0 / 5040 + z * (1.0 / 362880)))))
    c = 1.0 + z * (-0.5 + z * (1.0 / 24 + z * (-1.0 / 720 + z * (1.0 / 40320 + z * (-1.0 / 3628800)))))
    cm, sm = math.cos(mid), math.sin(mid)
    return s * cm + c * sm, c * cm - s * sm


def turned(x, back, size, axis):
    own = lax.broadcasted_iota(jnp.int32, x.shape, axis)
    return pltpu.roll(x, lax.rem(size - back, size), axis), own < size - back


def cut(ref, row, col, n):
    base = pl.multiple_of(row // SUB * SUB, SUB)
    groups = n // SUB + 1
    pieces = []
    for j in range(n // LANES + 1):
        x = ref[pl.ds(base, n + SUB), j * LANES : (j + 1) * LANES].reshape(groups, SUB, LANES)
        x, near = turned(x, row - base, SUB, 1)
        x = jnp.where(near[1:], x[:-1], x[1:]).reshape(n, LANES)
        pieces.append(turned(x, col, LANES, 1))
    return jnp.concatenate(
        [jnp.where(here[1], here[0], after[0]) for here, after in zip(pieces[:-1], pieces[1:])], axis=1
    )


def place(ref, row, col, block):
    n = block.shape[0]
    base = pl.multiple_of(row // SUB * SUB, SUB)
    groups = n // SUB
    zero = jnp.zeros((n, LANES), F32)
    pieces = [
        pltpu.roll(block[:, j * LANES : (j + 1) * LANES], lax.rem(col, LANES), 1) for j in range(n // LANES)
    ]
    far = lax.broadcasted_iota(jnp.int32, (n, LANES), 1) >= col
    gap = jnp.zeros((1, SUB, LANES), F32)
    low = lax.broadcasted_iota(jnp.int32, (groups + 1, SUB, LANES), 1) >= row - base
    for j, (before, here) in enumerate(zip([zero] + pieces, pieces + [zero])):
        x = jnp.where(far, here, before).reshape(groups, SUB, LANES)
        x = pltpu.roll(x, row - base, 1)
        x = jnp.where(low, jnp.concatenate([x, gap], 0), jnp.concatenate([gap, x], 0))
        spot = (pl.ds(base, n + SUB), slice(j * LANES, (j + 1) * LANES))
        ref[spot] = ref[spot] + x.reshape(n + SUB, LANES)


def right(real, imag, table):
    n = real.shape[1]
    both = jnp.concatenate([real.astype(BF16), imag.astype(BF16)], axis=1)
    out = jnp.dot(both, table[...], preferred_element_type=F32)
    return out[:, :n], out[:, n:]


def left(real, imag, table):
    n = real.shape[0]
    both = jnp.concatenate([real.astype(BF16), imag.astype(BF16)], axis=0)
    out = jnp.dot(table[...], both, preferred_element_type=F32)
    return out[:n], out[n:]


def forward(ur, ui, m, mt, pr, pi):
    ar, ai = right(ur, ui, mt)
    br, bi = left(ar, ai, m)
    return br * pr - bi * pi, br * pi + bi * pr


def inverse(fr, fi, m, mt):
    ar, ai = right(fr, fi, m)
    return left(ar, ai, mt)


def adjoint(lr, li, m, mt, pr, pi):
    ar, ai = right(lr, li, mt)
    br, bi = left(ar, ai, m)
    return inverse(br * pr + bi * pi, bi * pr - br * pi, m, mt)


def extent_kernel(pot, low, high, tr, ti):
    margin = low.shape[0]
    core = pot.shape[1]
    for rows, v in (
        (slice(0, margin), low[...].astype(F32)),
        (slice(margin, margin + core), pot[0]),
        (slice(margin + core, margin + core + margin), high[...].astype(F32)),
    ):
        s, c = sin_cos(SIGMA * v)
        tr[rows] = c
        ti[rows] = s


def first_adjoint_kernel(adj, m, mt, pr, pi, lr, li):
    lr[...], li[...] = adjoint(adj[0, 0, 0], adj[0, 0, 1], m, mt, pr[...], pi[...])


def step_kernel(tick, turn, gathered, *refs):
    first = tick == 0
    refs = list(refs)
    pos, tr, ti, saved, intens, m, mt, pr, pi = refs[:9]
    rest = refs[9:]
    fresh = first and turn == 1
    if first:
        fwd, lr0, li0 = rest[:3]
        rest = rest[3:]
    else:
        recv, probe = rest[:2]
        rest = rest[2:]
    if not fresh:
        rest = rest[1:]
    out, acc = rest
    n = out.shape[1]
    sections = lax.axis_size("depth")
    section = lax.axis_index("depth")
    parity = lax.rem(section, 2)
    is_forward = lax.rem(parity + tick, 2) == turn
    if fresh:
        acc[...] = jnp.zeros(acc.shape, F32)

    def received(part):
        return recv[1 - parity, part] if gathered else recv[part]

    @pl.when(is_forward)
    def _():
        mb = tick - section + 2 * sections - 1
        row, col = pos[mb, 0], pos[mb, 1]
        wr = cut(tr, row, col, n)
        wi = cut(ti, row, col, n)
        if first:
            xr, xi = fwd[0, 0, 0], fwd[0, 0, 1]
        else:
            xr, xi = received(0), received(1)
            if not gathered:
                at_start = section == 0
                xr = jnp.where(at_start, probe[0], xr)
                xi = jnp.where(at_start, probe[1], xi)
            xr, xi = xr.astype(F32), xi.astype(F32)
        fr, fi = forward(wr * xr - wi * xi, wr * xi + wi * xr, m, mt, pr[...], pi[...])
        excess = fr * fr + fi * fi - intens[0, tick].astype(F32)
        weight = jnp.where(section == sections - 1, excess, 1.0)
        sr, si = inverse(fr * weight, fi * weight, m, mt)
        out[0] = sr.astype(BF16)
        out[1] = si.astype(BF16)

    @pl.when(jnp.logical_not(is_forward))
    def _():
        mb = tick + section
        row, col = pos[mb, 0], pos[mb, 1]
        if first:
            lr, li = lr0[...], li0[...]
        else:
            lr, li = adjoint(received(0), received(1), m, mt, pr[...], pi[...])
        wr = cut(tr, row, col, n)
        wi = cut(ti, row, col, n)
        br = wr * lr + wi * li
        bi = wr * li - wi * lr
        out[0] = br.astype(BF16)
        out[1] = bi.astype(BF16)
        delta = SIGMA * (bi * saved[0, 0, tick, 0].astype(F32) - br * saved[0, 0, tick, 1].astype(F32))
        place(acc, row, col, delta)


def waves_kernel(swapped, gathered, probe, wave, adj):
    section = lax.axis_index("depth")
    parity = lax.rem(section, 2)

    @pl.when(parity == 0)
    def _():
        wave[0, 0] = jnp.where(section == 0, probe[...], swapped[...]).astype(F32)
        adj[0, 0] = gathered[1]

    @pl.when(parity == 1)
    def _():
        wave[0, 0] = gathered[0].astype(F32)
        adj[0, 0] = swapped[...]


def fold_kernel(acc, from_low, from_high, grad):
    margin = from_low.shape[0]
    core = grad.shape[1]
    grad[0, :margin] = acc[margin : 2 * margin] + from_low[...].astype(F32)
    grad[0, margin : core - margin] = acc[2 * margin : core]
    grad[0, core - margin :] = acc[core : core + margin] + from_high[...].astype(F32)


VM = pl.BlockSpec(memory_space=pltpu.VMEM)
SM = pl.BlockSpec(memory_space=pltpu.SMEM)


def call(kernel, name, in_specs, outs, args, aliases=None, cost=None, limit=24):
    return pl.pallas_call(
        kernel,
        name=name,
        in_specs=in_specs,
        out_specs=[VM] * len(outs),
        out_shape=outs,
        input_output_aliases=aliases or {},
        compiler_params=pltpu.CompilerParams(vmem_limit_bytes=limit << 20),
        cost_estimate=cost,
    )(*args)


def shape(*dims, dtype=F32):
    return jax.ShapeDtypeStruct(dims, dtype)


def swap_chips(x):
    last = lax.axis_size("depth") - 1
    route = [(0, 0), (last, last)]
    for i in range(1, last, 2):
        route += [(i, i + 1), (i + 1, i)]
    return lax.ppermute(x, "depth", route)


def gather_chip(x):
    count = lax.axis_size("depth")
    groups = [[i, i + 1] for i in range(0, count, 2)]
    return lax.all_gather(x, "depth", axis_index_groups=groups)


def tile_shift(x, distance):
    devices = range(lax.axis_size("tile"))
    route = [(i - distance, i) for i in devices if i - distance in devices]
    return lax.ppermute(x, "tile", route)


def on_device(potential, probe, positions, intensity, fwd_wave, adj_wave, saved_wave):
    n = probe.shape[1]
    core, cols = potential.shape[1:]
    margin = (cols - core) // 2
    tall = core + 2 * margin + SUB
    spots = positions[0]
    m, mt = (jnp.asarray(t) for t in dft_matrices(n))
    pr, pi = (jnp.asarray(t) for t in propagator(n))
    step_cost = pl.CostEstimate(flops=8 * 2 * n * n * n * 2, bytes_accessed=1 << 20, transcendentals=0)

    low = tile_shift(potential[0, core - margin :].astype(BF16), 1)
    high = tile_shift(potential[0, :margin].astype(BF16), -1)
    lr0, li0 = call(
        first_adjoint_kernel, "first_adjoint", [VM] * 5, [shape(n, n)] * 2, (adj_wave, m, mt, pr, pi), cost=step_cost
    )
    tr, ti = call(extent_kernel, "extent", [VM] * 3, [shape(tall, cols)] * 2, (potential, low, high))

    common = (spots, tr, ti, saved_wave, intensity, m, mt, pr, pi)
    outs = [shape(2, n, n, dtype=BF16), shape(tall, cols)]

    def start(turn, acc):
        args = common + (fwd_wave, lr0, li0) + (() if acc is None else (acc,))
        aliases = {} if acc is None else {len(args) - 1: 1}
        return call(
            functools.partial(step_kernel, 0, turn, False), f"step0_{turn}",
            [SM] + [VM] * (len(args) - 1), outs, args, aliases, step_cost,
        )

    def step(tick, turn, gathered, recv, acc):
        args = common + (recv, probe, acc)
        return call(
            functools.partial(step_kernel, tick, turn, gathered), f"step{tick}_{turn}",
            [SM] + [VM] * (len(args) - 1), outs, args, {len(args) - 1: 1}, step_cost,
        )

    b, acc = start(1, None)
    b = swap_chips(b)
    a, acc = start(0, acc)
    a = gather_chip(a)
    a, acc = step(1, 0, True, a, acc)
    a = swap_chips(a)
    b, acc = step(1, 1, False, b, acc)
    b = gather_chip(b)
    b, acc = step(2, 1, True, b, acc)
    b = swap_chips(b)
    a, acc = step(2, 0, False, a, acc)
    a = gather_chip(a)
    a, acc = step(3, 0, True, a, acc)
    a = swap_chips(a)
    b, acc = step(3, 1, False, b, acc)
    from_low = tile_shift(acc[margin + core : core + 2 * margin].astype(BF16), 1)
    from_high = tile_shift(acc[:margin].astype(BF16), -1)
    b = gather_chip(b)
    wave, adj = call(
        waves_kernel, "waves", [VM] * 3,
        [shape(1, 1, 2, n, n), shape(1, 1, 2, n, n, dtype=BF16)], (a, b, probe),
    )
    (grad,) = call(fold_kernel, "fold", [VM] * 3, [shape(1, core, cols)], (acc, from_low, from_high))
    return wave, adj, grad


def solution(mesh):
    placed = (
        P("depth", "tile", None),
        P(),
        P("tile", None, None),
        P("tile", None, None, None),
        P("depth", "tile", None, None, None),
        P("depth", "tile", None, None, None),
        P("depth", "tile", None, None, None, None),
    )
    return jax.shard_map(
        on_device,
        mesh=mesh,
        in_specs=placed,
        out_specs=(
            P("depth", "tile", None, None, None),
            P("depth", "tile", None, None, None),
            P("depth", "tile", None),
        ),
        check_vma=False,
    )
```

```python
import functools
import math

import jax
import jax.numpy as jnp
import numpy as np
from jax import lax
from jax.experimental import pallas as pl
from jax.experimental.pallas import tpu as pltpu
from jax.sharding import PartitionSpec as P

TICKS = 4
SIGMA = 0.8
DEFOCUS = 6.0
LANES = 128
SUB = 8
F32 = jnp.float32
BF16 = jnp.bfloat16


def dft_matrices(n):
    idx = np.arange(n)
    angle = ((idx[:, None] * idx[None, :]) % n).astype(np.float32) * np.float32(2.0 * math.pi / n)
    scale = np.float32(1.0 / math.sqrt(n))
    cos_t = np.cos(angle) * scale
    sin_t = np.sin(angle) * scale
    both = np.block([[cos_t, sin_t], [-sin_t, cos_t]])
    return both.astype(BF16), np.ascontiguousarray(both.T).astype(BF16)


def propagator(n):
    idx = np.arange(n)
    freq = np.where(idx < n // 2, idx, idx - n).astype(np.float32)
    square = freq[:, None] * freq[:, None] + freq[None, :] * freq[None, :]
    phase = np.float32(-math.pi * DEFOCUS) * square / np.float32(n * n)
    return np.cos(phase).astype(np.float32), np.sin(phase).astype(np.float32)


def sin_cos(x):
    mid = 1.2
    y = x - mid
    z = y * y
    s = y * (1.0 + z * (-1.0 / 6 + z * (1.0 / 120 + z * (-1.0 / 5040 + z * (1.0 / 362880)))))
    c = 1.0 + z * (-0.5 + z * (1.0 / 24 + z * (-1.0 / 720 + z * (1.0 / 40320 + z * (-1.0 / 3628800)))))
    cm, sm = math.cos(mid), math.sin(mid)
    return s * cm + c * sm, c * cm - s * sm


def turned(x, back, size, axis):
    own = lax.broadcasted_iota(jnp.int32, x.shape, axis)
    return pltpu.roll(x, lax.rem(size - back, size), axis), own < size - back


def cut(ref, row, col, n):
    base = pl.multiple_of(row // SUB * SUB, SUB)
    groups = n // SUB + 1
    pieces = []
    for j in range(n // LANES + 1):
        x = ref[pl.ds(base, n + SUB), j * LANES : (j + 1) * LANES].reshape(groups, SUB, LANES)
        x, near = turned(x, row - base, SUB, 1)
        x = jnp.where(near[1:], x[:-1], x[1:]).reshape(n, LANES)
        pieces.append(turned(x, col, LANES, 1))
    return jnp.concatenate(
        [jnp.where(here[1], here[0], after[0]) for here, after in zip(pieces[:-1], pieces[1:])], axis=1
    )


def place(ref, row, col, block):
    n = block.shape[0]
    base = pl.multiple_of(row // SUB * SUB, SUB)
    groups = n // SUB
    zero = jnp.zeros((n, LANES), F32)
    pieces = [
        pltpu.roll(block[:, j * LANES : (j + 1) * LANES], lax.rem(col, LANES), 1) for j in range(n // LANES)
    ]
    far = lax.broadcasted_iota(jnp.int32, (n, LANES), 1) >= col
    gap = jnp.zeros((1, SUB, LANES), F32)
    low = lax.broadcasted_iota(jnp.int32, (groups + 1, SUB, LANES), 1) >= row - base
    for j, (before, here) in enumerate(zip([zero] + pieces, pieces + [zero])):
        x = jnp.where(far, here, before).reshape(groups, SUB, LANES)
        x = pltpu.roll(x, row - base, 1)
        x = jnp.where(low, jnp.concatenate([x, gap], 0), jnp.concatenate([gap, x], 0))
        spot = (pl.ds(base, n + SUB), slice(j * LANES, (j + 1) * LANES))
        ref[spot] = ref[spot] + x.reshape(n + SUB, LANES)


def right(real, imag, table):
    n = real.shape[1]
    both = jnp.concatenate([real.astype(BF16), imag.astype(BF16)], axis=1)
    out = jnp.dot(both, table[...], preferred_element_type=F32)
    return out[:, :n], out[:, n:]


def left(real, imag, table):
    n = real.shape[0]
    both = jnp.concatenate([real.astype(BF16), imag.astype(BF16)], axis=0)
    out = jnp.dot(table[...], both, preferred_element_type=F32)
    return out[:n], out[n:]


def forward(ur, ui, m, mt, pr, pi):
    ar, ai = right(ur, ui, mt)
    br, bi = left(ar, ai, m)
    return br * pr - bi * pi, br * pi + bi * pr


def inverse(fr, fi, m, mt):
    ar, ai = right(fr, fi, m)
    return left(ar, ai, mt)


def adjoint(lr, li, m, mt, pr, pi):
    ar, ai = right(lr, li, mt)
    br, bi = left(ar, ai, m)
    return inverse(br * pr + bi * pi, bi * pr - br * pi, m, mt)


def edges_kernel(pot, low, high):
    margin = low.shape[0]
    core = pot.shape[1]
    low[...] = pot[0, core - margin :].astype(BF16)
    high[...] = pot[0, :margin].astype(BF16)


def transmit(v, tr, ti, rows):
    s, c = sin_cos(SIGMA * v)
    tr[rows] = c
    ti[rows] = s


def first_kernel(spots, pot, adj, m, mt, pr, pi, corners, lr, li, tr, ti):
    core = pot.shape[1]
    margin = (tr.shape[0] - SUB - core) // 2
    sections = lax.axis_size("depth")
    section = lax.axis_index("depth")
    which = lax.broadcasted_iota(jnp.int32, spots.shape, 1)
    for tick in range(TICKS):
        for backward, mb in enumerate((tick - section + 2 * sections - 1, tick + section)):
            at = 4 * tick + 2 * backward
            chosen = jnp.sum(jnp.where(which == mb, spots[...].astype(F32), 0.0), axis=1, keepdims=True)
            corners[at : at + 2] = jnp.broadcast_to(chosen.astype(jnp.int32), (2, LANES))
    lr[...], li[...] = adjoint(adj[0, 0, 0], adj[0, 0, 1], m, mt, pr[...], pi[...])
    transmit(pot[0], tr, ti, slice(margin, margin + core))


def corner(corners, tick, backward):
    at = 4 * tick + 2 * backward
    numbers = corners[...]
    return numbers[at, 0], numbers[at + 1, 0]


def step_kernel(tick, turn, *refs):
    first, fresh, last = tick == 0, tick == 0 and turn == 1, tick == TICKS - 1 and turn == 1
    gathered = tick > 0 and (tick + turn) % 2 == 1
    corners, saved, intens, m, mt, pr, pi, tr, ti, *rest = refs
    if first:
        fwd, lr0, li0, *rest = rest
    else:
        recv, probe, *rest = rest
    if fresh:
        low, high, out, acc, tr, ti = rest
    elif last:
        _, out, acc, to_low, to_high = rest
    else:
        _, out, acc = rest
    n = out.shape[1]
    sections = lax.axis_size("depth")
    section = lax.axis_index("depth")
    parity = lax.rem(section, 2)
    is_forward = lax.rem(parity + tick, 2) == turn
    if fresh:
        margin = low.shape[0]
        core = tr.shape[0] - SUB - 2 * margin
        transmit(low[...].astype(F32), tr, ti, slice(0, margin))
        transmit(high[...].astype(F32), tr, ti, slice(margin + core, 2 * margin + core))
        acc[...] = jnp.zeros(acc.shape, F32)

    def received(part):
        return recv[1 - parity, part] if gathered else recv[part]

    @pl.when(is_forward)
    def _():
        row, col = corner(corners, tick, 0)
        wr = cut(tr, row, col, n)
        wi = cut(ti, row, col, n)
        if first:
            xr, xi = fwd[0, 0, 0], fwd[0, 0, 1]
        else:
            xr, xi = received(0), received(1)
            if not gathered:
                at_start = section == 0
                xr = jnp.where(at_start, probe[0], xr)
                xi = jnp.where(at_start, probe[1], xi)
            xr, xi = xr.astype(F32), xi.astype(F32)
        fr, fi = forward(wr * xr - wi * xi, wr * xi + wi * xr, m, mt, pr[...], pi[...])
        excess = fr * fr + fi * fi - intens[0, tick].astype(F32)
        weight = jnp.where(section == sections - 1, excess, 1.0)
        sr, si = inverse(fr * weight, fi * weight, m, mt)
        out[0] = sr.astype(BF16)
        out[1] = si.astype(BF16)

    @pl.when(jnp.logical_not(is_forward))
    def _():
        row, col = corner(corners, tick, 1)
        if first:
            lr, li = lr0[...], li0[...]
        else:
            lr, li = adjoint(received(0), received(1), m, mt, pr[...], pi[...])
        wr = cut(tr, row, col, n)
        wi = cut(ti, row, col, n)
        br = wr * lr + wi * li
        bi = wr * li - wi * lr
        out[0] = br.astype(BF16)
        out[1] = bi.astype(BF16)
        delta = SIGMA * (bi * saved[0, 0, tick, 0].astype(F32) - br * saved[0, 0, tick, 1].astype(F32))
        place(acc, row, col, delta)

    if last:
        margin = to_low.shape[0]
        to_low[...] = acc[:margin].astype(BF16)
        to_high[...] = acc[acc.shape[0] - SUB - margin : acc.shape[0] - SUB].astype(BF16)


def finish_kernel(swapped, gathered, probe, acc, from_low, from_high, wave, adj, grad):
    section = lax.axis_index("depth")
    parity = lax.rem(section, 2)

    @pl.when(parity == 0)
    def _():
        wave[0, 0] = jnp.where(section == 0, probe[...], swapped[...]).astype(F32)
        adj[0, 0] = gathered[1]

    @pl.when(parity == 1)
    def _():
        wave[0, 0] = gathered[0].astype(F32)
        adj[0, 0] = swapped[...]

    margin = from_low.shape[0]
    core = grad.shape[1]
    grad[0, :margin] = acc[margin : 2 * margin] + from_low[...].astype(F32)
    grad[0, margin : core - margin] = acc[2 * margin : core]
    grad[0, core - margin :] = acc[core : core + margin] + from_high[...].astype(F32)


VM = pl.BlockSpec(memory_space=pltpu.VMEM)


def call(kernel, name, outs, args, aliases=None, cost=None):
    return pl.pallas_call(
        kernel,
        name=name,
        in_specs=[VM] * len(args),
        out_specs=[VM] * len(outs),
        out_shape=outs,
        input_output_aliases=aliases or {},
        compiler_params=pltpu.CompilerParams(vmem_limit_bytes=24 << 20),
        cost_estimate=cost,
    )(*args)


def shape(*dims, dtype=F32):
    return jax.ShapeDtypeStruct(dims, dtype)


def swap_chips(x):
    last = lax.axis_size("depth") - 1
    route = [(0, 0), (last, last)]
    for i in range(1, last, 2):
        route += [(i, i + 1), (i + 1, i)]
    return lax.ppermute(x, "depth", route)


def gather_chip(x):
    count = lax.axis_size("depth")
    groups = [[i, i + 1] for i in range(0, count, 2)]
    return lax.all_gather(x, "depth", axis_index_groups=groups)


def tile_shift(x, distance):
    devices = range(lax.axis_size("tile"))
    route = [(i - distance, i) for i in devices if i - distance in devices]
    return lax.ppermute(x, "tile", route)


def on_device(potential, probe, positions, intensity, fwd_wave, adj_wave, saved_wave):
    n = probe.shape[1]
    core, cols = potential.shape[1:]
    margin = (cols - core) // 2
    tall = core + 2 * margin + SUB
    spots = positions[0].T
    step_cost = pl.CostEstimate(flops=8 * 2 * n * n * n * 2, bytes_accessed=1 << 20, transcendentals=0)
    edge_cost = pl.CostEstimate(flops=1 << 33, bytes_accessed=1 << 20, transcendentals=0)
    extent = shape(tall, cols)
    edge = shape(margin, cols, dtype=BF16)
    half = shape(2, n, n, dtype=BF16)

    m, mt, pr, pi = (jnp.asarray(t) for t in (*dft_matrices(n), *propagator(n)))
    low, high = call(edges_kernel, "edges", [edge, edge], (potential,), cost=edge_cost)
    low = tile_shift(low, 1)
    high = tile_shift(high, -1)
    corners, lr0, li0, tr, ti = call(
        first_kernel, "first",
        [shape(4 * TICKS, LANES, dtype=jnp.int32)] + [shape(n, n)] * 2 + [extent] * 2,
        (spots, potential, adj_wave, m, mt, pr, pi), cost=step_cost,
    )
    common = (corners, saved_wave, intensity, m, mt, pr, pi)

    def step(tick, turn, extra, outs, aliases):
        args = (*common, tr, ti, *extra)
        return call(
            functools.partial(step_kernel, tick, turn), f"step{tick}_{turn}", [half, extent, *outs], args,
            {len(args) + i if i < 0 else i: o for i, o in aliases.items()}, step_cost,
        )

    def later(tick, turn, recv, acc, outs=()):
        return step(tick, turn, (recv, probe, acc), outs, {-1: 1})

    at_tr = len(common)
    b, acc, tr, ti = step(0, 1, (fwd_wave, lr0, li0, low, high), [extent, extent], {at_tr: 2, at_tr + 1: 3})
    b = swap_chips(b)
    a, acc = step(0, 0, (fwd_wave, lr0, li0, acc), (), {-1: 1})
    a = gather_chip(a)
    a, acc = later(1, 0, a, acc)
    a = swap_chips(a)
    b, acc = later(1, 1, b, acc)
    b = gather_chip(b)
    b, acc = later(2, 1, b, acc)
    b = swap_chips(b)
    a, acc = later(2, 0, a, acc)
    a = gather_chip(a)
    a, acc = later(3, 0, a, acc)
    a = swap_chips(a)
    b, acc, to_low, to_high = later(3, 1, b, acc, [edge, edge])
    from_low = tile_shift(to_high, 1)
    from_high = tile_shift(to_low, -1)
    b = gather_chip(b)
    return tuple(
        call(
            finish_kernel, "finish",
            [shape(1, 1, 2, n, n), shape(1, 1, 2, n, n, dtype=BF16), shape(1, core, cols)],
            (a, b, probe, acc, from_low, from_high),
        )
    )


def solution(mesh):
    placed = (
        P("depth", "tile", None),
        P(),
        P("tile", None, None),
        P("tile", None, None, None),
        P("depth", "tile", None, None, None),
        P("depth", "tile", None, None, None),
        P("depth", "tile", None, None, None, None),
    )
    return jax.shard_map(
        on_device,
        mesh=mesh,
        in_specs=placed,
        out_specs=(
            P("depth", "tile", None, None, None),
            P("depth", "tile", None, None, None),
            P("depth", "tile", None),
        ),
        check_vma=False,
    )
```

```python
import functools
import math

import jax
import jax.numpy as jnp
import numpy as np
from jax import lax
from jax.experimental import pallas as pl
from jax.experimental.pallas import tpu as pltpu
from jax.sharding import PartitionSpec as P

TICKS = 4
SIGMA = 0.8
DEFOCUS = 6.0
LANES = 128
SUB = 8
F32 = jnp.float32
BF16 = jnp.bfloat16


def halves(n):
    return np.concatenate([np.arange(0, n, 2), np.arange(1, n, 2)])


def dft_matrices(n):
    idx = np.arange(n)
    angle = ((idx[:, None] * idx[None, :]) % n).astype(np.float32) * np.float32(2.0 * math.pi / n)
    scale = np.float32(1.0 / math.sqrt(n))
    cos_t = np.cos(angle) * scale
    sin_t = np.sin(angle) * scale
    both = []
    for odd in range(2):
        c, s = cos_t[: n // 2, odd::2], sin_t[: n // 2, odd::2]
        both.append(np.block([[c, -s], [s, c]]))
    order = (halves(n)[:, None] == idx[None, :]).astype(np.float32)
    return np.stack([*both, both[0].T, both[1].T, order]).astype(BF16)


def propagator(n):
    freq = np.where(np.arange(n) < n // 2, np.arange(n), np.arange(n) - n).astype(np.float32)[halves(n)]
    square = freq[:, None] * freq[:, None] + freq[None, :] * freq[None, :]
    phase = np.float32(-math.pi * DEFOCUS) * square / np.float32(n * n)
    return np.stack([np.cos(phase), np.sin(phase)]).astype(np.float32)


def sin_cos(x):
    mid = 1.2
    y = x - mid
    z = y * y
    s = y * (1.0 + z * (-1.0 / 6 + z * (1.0 / 120 + z * (-1.0 / 5040 + z * (1.0 / 362880)))))
    c = 1.0 + z * (-0.5 + z * (1.0 / 24 + z * (-1.0 / 720 + z * (1.0 / 40320 + z * (-1.0 / 3628800)))))
    cm, sm = math.cos(mid), math.sin(mid)
    return s * cm + c * sm, c * cm - s * sm


def turned(x, back, size, axis):
    own = lax.broadcasted_iota(jnp.int32, x.shape, axis)
    return pltpu.roll(x, lax.rem(size - back, size), axis), own < size - back


def cut(ref, row, col, n):
    base = pl.multiple_of(row // SUB * SUB, SUB)
    groups = n // SUB + 1
    pieces = []
    for j in range(n // LANES + 1):
        x = ref[pl.ds(base, n + SUB), j * LANES : (j + 1) * LANES].reshape(groups, SUB, LANES)
        x, near = turned(x, row - base, SUB, 1)
        x = jnp.where(near[1:], x[:-1], x[1:]).reshape(n, LANES)
        pieces.append(turned(x, col, LANES, 1))
    return jnp.concatenate(
        [jnp.where(here[1], here[0], after[0]) for here, after in zip(pieces[:-1], pieces[1:])], axis=1
    )


def place(ref, row, col, block):
    n = block.shape[0]
    base = pl.multiple_of(row // SUB * SUB, SUB)
    groups = n // SUB
    zero = jnp.zeros((n, LANES), F32)
    pieces = [
        pltpu.roll(block[:, j * LANES : (j + 1) * LANES], lax.rem(col, LANES), 1) for j in range(n // LANES)
    ]
    far = lax.broadcasted_iota(jnp.int32, (n, LANES), 1) >= col
    gap = jnp.zeros((1, SUB, LANES), F32)
    low = lax.broadcasted_iota(jnp.int32, (groups + 1, SUB, LANES), 1) >= row - base
    for j, (before, here) in enumerate(zip([zero] + pieces, pieces + [zero])):
        x = jnp.where(far, here, before).reshape(groups, SUB, LANES)
        x = pltpu.roll(x, row - base, 1)
        x = jnp.where(low, jnp.concatenate([x, gap], 0), jnp.concatenate([gap, x], 0))
        spot = (pl.ds(base, n + SUB), slice(j * LANES, (j + 1) * LANES))
        ref[spot] = ref[spot] + x.reshape(n + SUB, LANES)


def dot(a, b):
    return jnp.dot(a, b, preferred_element_type=F32)


def beside(a, b):
    return jnp.concatenate([a.astype(BF16), b.astype(BF16)], axis=1)


def above(a, b):
    return jnp.concatenate([a.astype(BF16), b.astype(BF16)], axis=0)


def forward(xr, xi, tables):
    h = xr.shape[0] // 2
    xr, xi = xr.astype(F32), xi.astype(F32)
    even = dot(beside(xr[:, :h] + xr[:, h:], xi[:, :h] + xi[:, h:]), tables[0])
    odd = dot(beside(xr[:, :h] - xr[:, h:], xi[:, :h] - xi[:, h:]), tables[1])
    even_sum, even_gap = even[:h] + even[h:], even[:h] - even[h:]
    odd_sum, odd_gap = odd[:h] + odd[h:], odd[:h] - odd[h:]
    rows = []
    for table, e, o in ((2, even_sum, odd_sum), (3, even_gap, odd_gap)):
        rows.append(dot(tables[table], above(beside(e[:, :h], o[:, :h]), beside(e[:, h:], o[:, h:]))))
    return jnp.concatenate([r[:h] for r in rows], 0), jnp.concatenate([r[h:] for r in rows], 0)


def inverse(fr, fi, tables):
    h = fr.shape[0] // 2
    even = dot(beside(fr[:, :h], fi[:, :h]), tables[2])
    odd = dot(beside(fr[:, h:], fi[:, h:]), tables[3])
    low, high = even + odd, even - odd
    rows = []
    for table, at in ((0, slice(0, h)), (1, slice(h, 2 * h))):
        both = above(beside(low[at, :h], high[at, :h]), beside(low[at, h:], high[at, h:]))
        rows.append(dot(tables[table], both))
    even, odd = rows
    low, high = even + odd, even - odd
    return jnp.concatenate([low[:h], high[:h]], 0), jnp.concatenate([low[h:], high[h:]], 0)


def adjoint(lr, li, tables, prop):
    br, bi = forward(lr, li, tables)
    return inverse(br * prop[0] + bi * prop[1], bi * prop[0] - br * prop[1], tables)


def edges_kernel(pot, low, high):
    margin = low.shape[0]
    core = pot.shape[1]
    low[...] = pot[0, core - margin :].astype(BF16)
    high[...] = pot[0, :margin].astype(BF16)


def transmit(v, tr, ti, rows):
    s, c = sin_cos(SIGMA * v)
    tr[rows] = c
    ti[rows] = s


def window_of(section, tick, forward):
    return jnp.where(forward, tick - section + 2 * lax.axis_size("depth") - 1, tick + section)


def first_kernel(spots, pot, corners, tr, ti):
    core = pot.shape[1]
    margin = (tr.shape[0] - SUB - core) // 2
    section = lax.axis_index("depth")
    even = lax.rem(section, 2) == 0
    mate = jnp.where(even, section + 1, section - 1)
    which = lax.broadcasted_iota(jnp.int32, spots.shape, 1)
    windows = [window_of(section, 0, jnp.logical_not(even))]
    for tick in range(TICKS):
        windows += [window_of(section, tick, even), window_of(mate, tick, even)]
    windows[own(TICKS - 1)] = window_of(mate, TICKS - 1, jnp.logical_not(even))
    for i, mb in enumerate(windows):
        chosen = jnp.sum(jnp.where(which == mb, spots[...].astype(F32), 0.0), axis=1, keepdims=True)
        corners[2 * i : 2 * i + 2] = jnp.broadcast_to(chosen.astype(jnp.int32), (2, LANES))
    transmit(pot[0], tr, ti, slice(margin, margin + core))


def corner(corners, which):
    numbers = corners[...]
    return numbers[2 * which, 0], numbers[2 * which + 1, 0]


def own(tick):
    return 1 + 2 * tick


def mates(tick):
    return 2 + 2 * tick


def pack(ref, at, block):
    rows, n = block.shape[0], ref.shape[1]
    block = block.astype(BF16)
    ref[at : at + rows] = block[:, :n]
    ref[at + rows : at + rows + rows // 2, : n // 2] = block[: rows // 2, n:]
    ref[at + rows : at + rows + rows // 2, n // 2 :] = block[rows // 2 :, n:]


def unpack(rows, packed):
    n = packed.shape[1]
    return (
        (slice(0, rows), slice(0, n), packed[:rows]),
        (slice(0, rows // 2), slice(n, n + n // 2), packed[rows:, : n // 2]),
        (slice(rows // 2, rows), slice(n, n + n // 2), packed[rows:, n // 2 :]),
    )


def share_kernel(low, high, pot, saved, tr0, ti0, tr, ti, shared):
    margin = low.shape[0]
    core = pot.shape[1]
    transmit(low[...].astype(F32), tr, ti, slice(0, margin))
    transmit(high[...].astype(F32), tr, ti, slice(margin + core, 2 * margin + core))
    n = shared.shape[1]
    for tick in range(1, TICKS):
        for part in range(2):
            at = (2 * (tick - 1) + part) * n
            shared[at : at + n] = saved[0, 0, tick, part]
    whole = jnp.concatenate([low[...], pot[0].astype(BF16), high[...]], axis=0)
    pack(shared, 2 * (TICKS - 1) * n, whole)


def forward_step(xr, xi, section, tick, spot, tr, ti, intens, tables, prop, far):
    n = far.shape[1]
    wr = cut(tr, *spot, n)
    wi = cut(ti, *spot, n)
    xr, xi = xr.astype(F32), xi.astype(F32)
    br, bi = forward(wr * xr - wi * xi, wr * xi + wi * xr, tables)
    far[0] = br * prop[0] - bi * prop[1]
    far[1] = br * prop[1] + bi * prop[0]

    @pl.when(section == lax.axis_size("depth") - 1)
    def _():
        rows = dot(tables[4], intens[0, tick]).astype(BF16)
        ordered = lax.dot_general(rows, tables[4], (((1,), (1,)), ((), ())), preferred_element_type=F32)
        fr, fi = far[0], far[1]
        excess = fr * fr + fi * fi - ordered
        far[0] = excess * fr
        far[1] = excess * fi

    sr, si = inverse(far[0], far[1], tables)
    return sr.astype(BF16), si.astype(BF16)


def backward_step(lr, li, saved, spot, tr, ti, acc):
    n = lr.shape[0]
    wr = cut(tr, *spot, n)
    wi = cut(ti, *spot, n)
    br = wr * lr + wi * li
    bi = wr * li - wi * lr
    place(acc, *spot, SIGMA * (bi * saved[0].astype(F32) - br * saved[1].astype(F32)))
    return br.astype(BF16), bi.astype(BF16)


def entering(recv, probe, section):
    at_start = section == 0
    return [jnp.where(at_start, probe[part], recv[part]) for part in range(2)]


def first_step_kernel(corners, saved, intens, tables, prop, tr, ti, fwd, adj, out, acc, far):
    section = lax.axis_index("depth")
    even = lax.rem(section, 2) == 0
    spot = corner(corners, 0)
    acc[...] = jnp.zeros(acc.shape, F32)

    @pl.when(jnp.logical_not(even))
    def _():
        x = fwd[0, 0, 0], fwd[0, 0, 1]
        out[0], out[1] = forward_step(*x, section, 0, spot, tr, ti, intens, tables, prop, far)

    @pl.when(even)
    def _():
        theirs = saved[0, 0, 0, 0], saved[0, 0, 0, 1]
        x = adjoint(adj[0, 0, 0], adj[0, 0, 1], tables, prop)
        out[0], out[1] = backward_step(*x, theirs, spot, tr, ti, acc)


def last_step_kernel(corners, intens, tables, prop, mate_tr, mate_ti, shared, recv, probe, acc0, out, acc, packed, far):
    tick = TICKS - 1
    section = lax.axis_index("depth")
    even = lax.rem(section, 2) == 0
    n = far.shape[1]
    spot = corner(corners, own(tick))

    @pl.when(jnp.logical_not(even))
    def _():
        x = entering(recv, probe, section - 1)
        x = forward_step(*x, section - 1, tick, spot, mate_tr, mate_ti, intens, tables, prop, far)
        out[0], out[1] = x

    @pl.when(even)
    def _():
        x = adjoint(recv[0], recv[1], tables, prop)
        at = 2 * (tick - 1) * n
        theirs = shared[at : at + n], shared[at + n : at + 2 * n]
        out[0], out[1] = backward_step(*x, theirs, spot, mate_tr, mate_ti, acc)

    pack(packed, 0, acc[: acc.shape[0] - SUB])


def pair_kernel(tick, fresh, corners, saved, intens, tables, prop, tr, ti, shared, *refs):
    if fresh:
        fwd, adj, _, out, acc, mate_acc, mate_tr, mate_ti, far = refs
    else:
        recv, probe, mate_tr, mate_ti, _, _, out, acc, mate_acc, far = refs
    section = lax.axis_index("depth")
    even = lax.rem(section, 2) == 0
    n = far.shape[1]
    spot, mate_spot = corner(corners, own(tick)), corner(corners, mates(tick + 1))
    if fresh:
        rows = mate_tr.shape[0] - SUB
        for where_rows, where_columns, v in unpack(rows, shared[2 * (TICKS - 1) * n :]):
            s, c = sin_cos(SIGMA * v.astype(F32))
            mate_tr[where_rows, where_columns] = c
            mate_ti[where_rows, where_columns] = s
        mate_acc[...] = jnp.zeros(mate_acc.shape, F32)

    @pl.when(even)
    def _():
        x = (fwd[0, 0, 0], fwd[0, 0, 1]) if fresh else entering(recv, probe, section)
        x = forward_step(*x, section, tick, spot, tr, ti, intens, tables, prop, far)
        x = forward_step(*x, section + 1, tick + 1, mate_spot, mate_tr, mate_ti, intens, tables, prop, far)
        out[0], out[1] = x

    @pl.when(jnp.logical_not(even))
    def _():
        x = (adj[0, 0, 0], adj[0, 0, 1]) if fresh else (recv[0], recv[1])
        x = adjoint(*x, tables, prop)
        x = backward_step(*x, (saved[0, 0, tick, 0], saved[0, 0, tick, 1]), spot, tr, ti, acc)
        x = adjoint(*x, tables, prop)
        at = 2 * tick * n
        theirs = shared[at : at + n], shared[at + n : at + 2 * n]
        x = backward_step(*x, theirs, mate_spot, mate_tr, mate_ti, mate_acc)
        out[0], out[1] = x


def sum_kernel(gathered, acc0, low, high, acc):
    other = 1 - lax.rem(lax.axis_index("depth"), 2)
    rows = acc.shape[0] - SUB
    margin = low.shape[0]
    for where_rows, where_columns, part in unpack(rows, gathered[other]):
        acc[where_rows, where_columns] += part.astype(F32)
    low[...] = acc[:margin].astype(BF16)
    high[...] = acc[rows - margin : rows].astype(BF16)


def waves_kernel(swapped, stayed, probe, wave, adj):
    section = lax.axis_index("depth")
    even = lax.rem(section, 2) == 0

    @pl.when(even)
    def _():
        wave[0, 0] = jnp.where(section == 0, probe[...], swapped[...]).astype(F32)
        adj[0, 0] = stayed[...]

    @pl.when(jnp.logical_not(even))
    def _():
        wave[0, 0] = stayed[...].astype(F32)
        adj[0, 0] = swapped[...]


def fold_kernel(acc, from_low, from_high, grad):
    margin = from_low.shape[0]
    core = grad.shape[1]
    grad[0, :margin] = acc[margin : 2 * margin] + from_low[...].astype(F32)
    grad[0, margin : core - margin] = acc[2 * margin : core]
    grad[0, core - margin :] = acc[core : core + margin] + from_high[...].astype(F32)


VM = pl.BlockSpec(memory_space=pltpu.VMEM)


def call(kernel, name, outs, args, aliases=None, cost=None, scratch=()):
    return pl.pallas_call(
        kernel,
        name=name,
        in_specs=[VM] * len(args),
        out_specs=[VM] * len(outs),
        out_shape=outs,
        scratch_shapes=scratch,
        input_output_aliases=aliases or {},
        compiler_params=pltpu.CompilerParams(vmem_limit_bytes=24 << 20),
        cost_estimate=cost,
    )(*args)


def shape(*dims, dtype=F32):
    return jax.ShapeDtypeStruct(dims, dtype)


def swap_chips(x):
    last = lax.axis_size("depth") - 1
    route = [(0, 0), (last, last)]
    for i in range(1, last, 2):
        route += [(i, i + 1), (i + 1, i)]
    return lax.ppermute(x, "depth", route)


def ring(x):
    last = lax.axis_size("depth") - 1
    route = [(last - 1, last), (1, 0)]
    for i in range(0, last - 1, 2):
        route += [(i, i + 2), (i + 3, i + 1)]
    return lax.ppermute(x, "depth", route)


def cross(x):
    last = lax.axis_size("depth") - 1
    route = [(last - 1, last - 1), (1, 1)]
    for i in range(0, last - 1, 2):
        route += [(i, i + 3), (i + 3, i)]
    return lax.ppermute(x, "depth", route)


def swap_cores(x):
    return lax.ppermute(x, "depth", [(i, i ^ 1) for i in range(lax.axis_size("depth"))])


def gather_chip(x):
    count = lax.axis_size("depth")
    groups = [[i, i + 1] for i in range(0, count, 2)]
    return lax.all_gather(x, "depth", axis_index_groups=groups)


def tile_shift(x, distance):
    devices = range(lax.axis_size("tile"))
    route = [(i - distance, i) for i in devices if i - distance in devices]
    return lax.ppermute(x, "tile", route)


def on_device(potential, probe, positions, intensity, fwd_wave, adj_wave, saved_wave):
    n = probe.shape[1]
    core, cols = potential.shape[1:]
    margin = (cols - core) // 2
    tall = core + 2 * margin + SUB
    spots = positions[0].T
    step_cost = pl.CostEstimate(flops=8 * 2 * n * n * n * 2, bytes_accessed=1 << 20, transcendentals=0)
    pair_cost = pl.CostEstimate(flops=2 * 8 * 2 * n * n * n * 2, bytes_accessed=1 << 20, transcendentals=0)
    edge_cost = pl.CostEstimate(flops=1 << 33, bytes_accessed=1 << 20, transcendentals=0)
    far = [pltpu.VMEM((2, n, n), F32)]
    extent = shape(tall, cols)
    edge = shape(margin, cols, dtype=BF16)
    half = shape(2, n, n, dtype=BF16)

    tables, prop = jnp.asarray(dft_matrices(n)), jnp.asarray(propagator(n))
    low, high = call(edges_kernel, "edges", [edge, edge], (potential,), cost=edge_cost)
    low = tile_shift(low, 1)
    high = tile_shift(high, -1)
    corners, tr, ti = call(
        first_kernel, "first", [shape(4 * TICKS + 8, LANES, dtype=jnp.int32), extent, extent], (spots, potential),
        cost=step_cost,
    )
    packed = (tall - SUB) * 3 // 2
    tr, ti, shared = call(
        share_kernel, "share", [extent] * 2 + [shape(2 * (TICKS - 1) * n + packed, n, dtype=BF16)],
        (low, high, potential, saved_wave, tr, ti), {4: 0, 5: 1},
    )
    shared = swap_cores(shared)
    common = (corners, saved_wave, intensity, tables, prop, tr, ti)
    entry = (fwd_wave, adj_wave)

    b, acc = call(first_step_kernel, "step0", [half, extent], common + entry, cost=step_cost, scratch=far)
    b = swap_chips(b)
    args = (*common, shared, *entry, acc)
    a, acc, mate_acc, mate_tr, mate_ti = call(
        functools.partial(pair_kernel, 0, True), "steps01", [half] + [extent] * 4, args, {len(args) - 1: 1}, pair_cost, far
    )
    a = ring(a)

    def pair(tick, recv, acc, mate_acc):
        args = (*common, shared, recv, probe, mate_tr, mate_ti, acc, mate_acc)
        return call(
            functools.partial(pair_kernel, tick, False), f"steps{tick}{tick + 1}", [half, extent, extent], args,
            {len(args) - 2: 1, len(args) - 1: 2}, pair_cost, far,
        )

    b, acc, mate_acc = pair(1, b, acc, mate_acc)
    b = cross(b)
    a, acc, mate_acc = pair(2, a, acc, mate_acc)
    a = ring(a)
    args = (corners, intensity, tables, prop, mate_tr, mate_ti, shared, b, probe, mate_acc)
    b, mate_acc, mate_sum = call(
        last_step_kernel, "step3", [half, extent, shape(packed, n, dtype=BF16)], args, {len(args) - 1: 1}, step_cost, far
    )
    to_low, to_high, acc = call(sum_kernel, "sum", [edge, edge, extent], (gather_chip(mate_sum), acc), {1: 2})
    from_low = tile_shift(to_high, 1)
    from_high = tile_shift(to_low, -1)
    wave, adj = call(
        waves_kernel, "waves", [shape(1, 1, 2, n, n), shape(1, 1, 2, n, n, dtype=BF16)], (a, b, probe)
    )
    acc, wave, adj = lax.optimization_barrier((acc, wave, adj))
    (grad,) = call(fold_kernel, "fold", [shape(1, core, cols)], (acc, from_low, from_high))
    return wave, adj, grad


def solution(mesh):
    placed = (
        P("depth", "tile", None),
        P(),
        P("tile", None, None),
        P("tile", None, None, None),
        P("depth", "tile", None, None, None),
        P("depth", "tile", None, None, None),
        P("depth", "tile", None, None, None, None),
    )
    return jax.shard_map(
        on_device,
        mesh=mesh,
        in_specs=placed,
        out_specs=(
            P("depth", "tile", None, None, None),
            P("depth", "tile", None, None, None),
            P("depth", "tile", None),
        ),
        check_vma=False,
    )
```

```python
import functools
import math

import jax
import jax.numpy as jnp
import numpy as np
from jax import lax
from jax.experimental import pallas as pl
from jax.experimental.pallas import tpu as pltpu
from jax.sharding import PartitionSpec as P

TICKS = 4
SIGMA = 0.8
DEFOCUS = 6.0
LANES = 128
SUB = 8
F32 = jnp.float32
BF16 = jnp.bfloat16


def halves(n):
    return np.concatenate([np.arange(0, n, 2), np.arange(1, n, 2)])


def dft_matrices(n):
    idx = np.arange(n)
    angle = ((idx[:, None] * idx[None, :]) % n).astype(np.float32) * np.float32(2.0 * math.pi / n)
    scale = np.float32(1.0 / math.sqrt(n))
    cos_t = np.cos(angle) * scale
    sin_t = np.sin(angle) * scale
    both = []
    for odd in range(2):
        c, s = cos_t[: n // 2, odd::2], sin_t[: n // 2, odd::2]
        both.append(np.block([[c, -s], [s, c]]))
    order = (halves(n)[:, None] == idx[None, :]).astype(np.float32)
    return np.stack([*both, both[0].T, both[1].T, order]).astype(BF16)


def propagator(n):
    freq = np.where(np.arange(n) < n // 2, np.arange(n), np.arange(n) - n).astype(np.float32)[halves(n)]
    square = freq[:, None] * freq[:, None] + freq[None, :] * freq[None, :]
    phase = np.float32(-math.pi * DEFOCUS) * square / np.float32(n * n)
    return np.stack([np.cos(phase), np.sin(phase)]).astype(np.float32)


def sin_cos(x):
    mid = 1.2
    y = x - mid
    z = y * y
    s = y * (1.0 + z * (-1.0 / 6 + z * (1.0 / 120 + z * (-1.0 / 5040 + z * (1.0 / 362880)))))
    c = 1.0 + z * (-0.5 + z * (1.0 / 24 + z * (-1.0 / 720 + z * (1.0 / 40320 + z * (-1.0 / 3628800)))))
    cm, sm = math.cos(mid), math.sin(mid)
    return s * cm + c * sm, c * cm - s * sm


def turned(x, back, size, axis):
    own = lax.broadcasted_iota(jnp.int32, x.shape, axis)
    return pltpu.roll(x, lax.rem(size - back, size), axis), own < size - back


def cut(ref, row, col, n):
    base = pl.multiple_of(row // SUB * SUB, SUB)
    groups = n // SUB + 1
    pieces = []
    for j in range(n // LANES + 1):
        x = ref[pl.ds(base, n + SUB), j * LANES : (j + 1) * LANES].reshape(groups, SUB, LANES)
        x, near = turned(x, row - base, SUB, 1)
        x = jnp.where(near[1:], x[:-1], x[1:]).reshape(n, LANES)
        pieces.append(turned(x, col, LANES, 1))
    return jnp.concatenate(
        [jnp.where(here[1], here[0], after[0]) for here, after in zip(pieces[:-1], pieces[1:])], axis=1
    )


def place(ref, row, col, block):
    n = block.shape[0]
    base = pl.multiple_of(row // SUB * SUB, SUB)
    groups = n // SUB
    zero = jnp.zeros((n, LANES), F32)
    pieces = [
        pltpu.roll(block[:, j * LANES : (j + 1) * LANES], lax.rem(col, LANES), 1) for j in range(n // LANES)
    ]
    far = lax.broadcasted_iota(jnp.int32, (n, LANES), 1) >= col
    gap = jnp.zeros((1, SUB, LANES), F32)
    low = lax.broadcasted_iota(jnp.int32, (groups + 1, SUB, LANES), 1) >= row - base
    for j, (before, here) in enumerate(zip([zero] + pieces, pieces + [zero])):
        x = jnp.where(far, here, before).reshape(groups, SUB, LANES)
        x = pltpu.roll(x, row - base, 1)
        x = jnp.where(low, jnp.concatenate([x, gap], 0), jnp.concatenate([gap, x], 0))
        spot = (pl.ds(base, n + SUB), slice(j * LANES, (j + 1) * LANES))
        ref[spot] = ref[spot] + x.reshape(n + SUB, LANES)


def dot(a, b):
    return jnp.dot(a, b, preferred_element_type=F32)


def beside(a, b):
    return jnp.concatenate([a.astype(BF16), b.astype(BF16)], axis=1)


def above(a, b):
    return jnp.concatenate([a.astype(BF16), b.astype(BF16)], axis=0)


def forward(xr, xi, tables):
    h = xr.shape[0] // 2
    xr, xi = xr.astype(F32), xi.astype(F32)
    even = dot(beside(xr[:, :h] + xr[:, h:], xi[:, :h] + xi[:, h:]), tables[0])
    odd = dot(beside(xr[:, :h] - xr[:, h:], xi[:, :h] - xi[:, h:]), tables[1])
    even_sum, even_gap = even[:h] + even[h:], even[:h] - even[h:]
    odd_sum, odd_gap = odd[:h] + odd[h:], odd[:h] - odd[h:]
    rows = []
    for table, e, o in ((2, even_sum, odd_sum), (3, even_gap, odd_gap)):
        rows.append(dot(tables[table], above(beside(e[:, :h], o[:, :h]), beside(e[:, h:], o[:, h:]))))
    return jnp.concatenate([r[:h] for r in rows], 0), jnp.concatenate([r[h:] for r in rows], 0)


def inverse(fr, fi, tables):
    h = fr.shape[0] // 2
    even = dot(beside(fr[:, :h], fi[:, :h]), tables[2])
    odd = dot(beside(fr[:, h:], fi[:, h:]), tables[3])
    low, high = even + odd, even - odd
    rows = []
    for table, at in ((0, slice(0, h)), (1, slice(h, 2 * h))):
        both = above(beside(low[at, :h], high[at, :h]), beside(low[at, h:], high[at, h:]))
        rows.append(dot(tables[table], both))
    even, odd = rows
    low, high = even + odd, even - odd
    return jnp.concatenate([low[:h], high[:h]], 0), jnp.concatenate([low[h:], high[h:]], 0)


def adjoint(lr, li, tables, prop):
    br, bi = forward(lr, li, tables)
    return inverse(br * prop[0] + bi * prop[1], bi * prop[0] - br * prop[1], tables)


def odd_tile():
    return lax.rem(lax.axis_index("tile"), 2) == 1


def edges_kernel(pot, inner, outer):
    margin = inner.shape[0]
    core = pot.shape[1]
    low = pot[0, :margin].astype(BF16)
    high = pot[0, core - margin :].astype(BF16)
    inner[...] = jnp.where(odd_tile(), high, low)
    outer[...] = jnp.where(odd_tile(), low, high)


def transmit(v, tr, ti, rows):
    s, c = sin_cos(SIGMA * v)
    tr[rows] = c
    ti[rows] = s


def window_of(section, tick, forward):
    return jnp.where(forward, tick - section + 2 * lax.axis_size("depth") - 1, tick + section)


def first_kernel(spots, pot, corners, tr, ti):
    core = pot.shape[1]
    margin = (tr.shape[0] - SUB - core) // 2
    section = lax.axis_index("depth")
    even = lax.rem(section, 2) == 0
    mate = jnp.where(even, section + 1, section - 1)
    which = lax.broadcasted_iota(jnp.int32, spots.shape, 1)
    windows = [window_of(section, 0, jnp.logical_not(even))]
    for tick in range(TICKS):
        windows += [window_of(section, tick, even), window_of(mate, tick, even)]
    windows[own(TICKS - 1)] = window_of(mate, TICKS - 1, jnp.logical_not(even))
    for i, mb in enumerate(windows):
        chosen = jnp.sum(jnp.where(which == mb, spots[...].astype(F32), 0.0), axis=1, keepdims=True)
        corners[2 * i : 2 * i + 2] = jnp.broadcast_to(chosen.astype(jnp.int32), (2, LANES))
    transmit(pot[0], tr, ti, slice(margin, margin + core))


def corner(corners, which):
    numbers = corners[...]
    return numbers[2 * which, 0], numbers[2 * which + 1, 0]


def own(tick):
    return 1 + 2 * tick


def mates(tick):
    return 2 + 2 * tick


def pack(ref, at, block):
    rows, n = block.shape[0], ref.shape[1]
    block = block.astype(BF16)
    ref[at : at + rows] = block[:, :n]
    ref[at + rows : at + rows + rows // 2, : n // 2] = block[: rows // 2, n:]
    ref[at + rows : at + rows + rows // 2, n // 2 :] = block[rows // 2 :, n:]


def unpack(rows, packed):
    n = packed.shape[1]
    return (
        (slice(0, rows), slice(0, n), packed[:rows]),
        (slice(0, rows // 2), slice(n, n + n // 2), packed[rows:, : n // 2]),
        (slice(rows // 2, rows), slice(n, n + n // 2), packed[rows:, n // 2 :]),
    )


def share_kernel(inner, outer, pot, saved, tr0, ti0, tr, ti, shared):
    margin = inner.shape[0]
    core = pot.shape[1]
    low = jnp.where(odd_tile(), outer[...], inner[...])
    high = jnp.where(odd_tile(), inner[...], outer[...])
    transmit(low.astype(F32), tr, ti, slice(0, margin))
    transmit(high.astype(F32), tr, ti, slice(margin + core, 2 * margin + core))
    n = shared.shape[1]
    for tick in range(1, TICKS):
        for part in range(2):
            at = (2 * (tick - 1) + part) * n
            shared[at : at + n] = saved[0, 0, tick, part]
    whole = jnp.concatenate([low, pot[0].astype(BF16), high], axis=0)
    pack(shared, 2 * (TICKS - 1) * n, whole)


def forward_step(xr, xi, section, tick, spot, tr, ti, intens, tables, prop, far):
    n = far.shape[1]
    wr = cut(tr, *spot, n)
    wi = cut(ti, *spot, n)
    xr, xi = xr.astype(F32), xi.astype(F32)
    br, bi = forward(wr * xr - wi * xi, wr * xi + wi * xr, tables)
    far[0] = br * prop[0] - bi * prop[1]
    far[1] = br * prop[1] + bi * prop[0]

    @pl.when(section == lax.axis_size("depth") - 1)
    def _():
        rows = dot(tables[4], intens[0, tick]).astype(BF16)
        ordered = lax.dot_general(rows, tables[4], (((1,), (1,)), ((), ())), preferred_element_type=F32)
        fr, fi = far[0], far[1]
        excess = fr * fr + fi * fi - ordered
        far[0] = excess * fr
        far[1] = excess * fi

    sr, si = inverse(far[0], far[1], tables)
    return sr.astype(BF16), si.astype(BF16)


def backward_step(lr, li, saved, spot, tr, ti, acc):
    n = lr.shape[0]
    wr = cut(tr, *spot, n)
    wi = cut(ti, *spot, n)
    br = wr * lr + wi * li
    bi = wr * li - wi * lr
    place(acc, *spot, SIGMA * (bi * saved[0].astype(F32) - br * saved[1].astype(F32)))
    return br.astype(BF16), bi.astype(BF16)


def entering(recv, probe, section):
    at_start = section == 0
    return [jnp.where(at_start, probe[part], recv[part]) for part in range(2)]


def first_step_kernel(corners, saved, intens, tables, prop, tr, ti, fwd, adj, out, acc, far):
    section = lax.axis_index("depth")
    even = lax.rem(section, 2) == 0
    spot = corner(corners, 0)
    acc[...] = jnp.zeros(acc.shape, F32)

    @pl.when(jnp.logical_not(even))
    def _():
        x = fwd[0, 0, 0], fwd[0, 0, 1]
        out[0], out[1] = forward_step(*x, section, 0, spot, tr, ti, intens, tables, prop, far)

    @pl.when(even)
    def _():
        theirs = saved[0, 0, 0, 0], saved[0, 0, 0, 1]
        x = adjoint(adj[0, 0, 0], adj[0, 0, 1], tables, prop)
        out[0], out[1] = backward_step(*x, theirs, spot, tr, ti, acc)


def last_step_kernel(corners, intens, tables, prop, mate_tr, mate_ti, shared, recv, probe, acc0, out, acc, packed, far):
    tick = TICKS - 1
    section = lax.axis_index("depth")
    even = lax.rem(section, 2) == 0
    n = far.shape[1]
    spot = corner(corners, own(tick))

    @pl.when(jnp.logical_not(even))
    def _():
        x = entering(recv, probe, section - 1)
        x = forward_step(*x, section - 1, tick, spot, mate_tr, mate_ti, intens, tables, prop, far)
        out[0], out[1] = x

    @pl.when(even)
    def _():
        x = adjoint(recv[0], recv[1], tables, prop)
        at = 2 * (tick - 1) * n
        theirs = shared[at : at + n], shared[at + n : at + 2 * n]
        out[0], out[1] = backward_step(*x, theirs, spot, mate_tr, mate_ti, acc)

    pack(packed, 0, acc[: acc.shape[0] - SUB])


def pair_kernel(tick, fresh, corners, saved, intens, tables, prop, tr, ti, shared, *refs):
    if fresh:
        fwd, adj, _, out, acc, mate_acc, mate_tr, mate_ti, far = refs
    else:
        recv, probe, mate_tr, mate_ti, _, _, out, acc, mate_acc, far = refs
    section = lax.axis_index("depth")
    even = lax.rem(section, 2) == 0
    n = far.shape[1]
    spot, mate_spot = corner(corners, own(tick)), corner(corners, mates(tick + 1))
    if fresh:
        rows = mate_tr.shape[0] - SUB
        for where_rows, where_columns, v in unpack(rows, shared[2 * (TICKS - 1) * n :]):
            s, c = sin_cos(SIGMA * v.astype(F32))
            mate_tr[where_rows, where_columns] = c
            mate_ti[where_rows, where_columns] = s
        mate_acc[...] = jnp.zeros(mate_acc.shape, F32)

    @pl.when(even)
    def _():
        x = (fwd[0, 0, 0], fwd[0, 0, 1]) if fresh else entering(recv, probe, section)
        x = forward_step(*x, section, tick, spot, tr, ti, intens, tables, prop, far)
        x = forward_step(*x, section + 1, tick + 1, mate_spot, mate_tr, mate_ti, intens, tables, prop, far)
        out[0], out[1] = x

    @pl.when(jnp.logical_not(even))
    def _():
        x = (adj[0, 0, 0], adj[0, 0, 1]) if fresh else (recv[0], recv[1])
        x = adjoint(*x, tables, prop)
        x = backward_step(*x, (saved[0, 0, tick, 0], saved[0, 0, tick, 1]), spot, tr, ti, acc)
        x = adjoint(*x, tables, prop)
        at = 2 * tick * n
        theirs = shared[at : at + n], shared[at + n : at + 2 * n]
        x = backward_step(*x, theirs, mate_spot, mate_tr, mate_ti, mate_acc)
        out[0], out[1] = x


def sum_kernel(gathered, acc0, inner, outer, acc):
    other = 1 - lax.rem(lax.axis_index("depth"), 2)
    rows = acc.shape[0] - SUB
    margin = inner.shape[0]
    for where_rows, where_columns, part in unpack(rows, gathered[other]):
        acc[where_rows, where_columns] += part.astype(F32)
    low = acc[:margin].astype(BF16)
    high = acc[rows - margin : rows].astype(BF16)
    inner[...] = jnp.where(odd_tile(), high, low)
    outer[...] = jnp.where(odd_tile(), low, high)


def waves_kernel(swapped, stayed, probe, wave, adj):
    section = lax.axis_index("depth")
    even = lax.rem(section, 2) == 0

    @pl.when(even)
    def _():
        wave[0, 0] = jnp.where(section == 0, probe[...], swapped[...]).astype(F32)
        adj[0, 0] = stayed[...]

    @pl.when(jnp.logical_not(even))
    def _():
        wave[0, 0] = stayed[...].astype(F32)
        adj[0, 0] = swapped[...]


def fold_kernel(acc, inner, outer, grad):
    margin = inner.shape[0]
    core = grad.shape[1]
    from_low = jnp.where(odd_tile(), outer[...], inner[...])
    from_high = jnp.where(odd_tile(), inner[...], outer[...])
    grad[0, :margin] = acc[margin : 2 * margin] + from_low.astype(F32)
    grad[0, margin : core - margin] = acc[2 * margin : core]
    grad[0, core - margin :] = acc[core : core + margin] + from_high.astype(F32)


VM = pl.BlockSpec(memory_space=pltpu.VMEM)


def call(kernel, name, outs, args, aliases=None, cost=None, scratch=()):
    return pl.pallas_call(
        kernel,
        name=name,
        in_specs=[VM] * len(args),
        out_specs=[VM] * len(outs),
        out_shape=outs,
        scratch_shapes=scratch,
        input_output_aliases=aliases or {},
        compiler_params=pltpu.CompilerParams(vmem_limit_bytes=24 << 20),
        cost_estimate=cost,
    )(*args)


def shape(*dims, dtype=F32):
    return jax.ShapeDtypeStruct(dims, dtype)


def swap_chips(x):
    last = lax.axis_size("depth") - 1
    route = [(0, 0), (last, last)]
    for i in range(1, last, 2):
        route += [(i, i + 1), (i + 1, i)]
    return lax.ppermute(x, "depth", route)


def ring(x):
    last = lax.axis_size("depth") - 1
    route = [(last - 1, last), (1, 0)]
    for i in range(0, last - 1, 2):
        route += [(i, i + 2), (i + 3, i + 1)]
    return lax.ppermute(x, "depth", route)


def cross(x):
    last = lax.axis_size("depth") - 1
    route = [(last - 1, last - 1), (1, 1)]
    for i in range(0, last - 1, 2):
        route += [(i, i + 3), (i + 3, i)]
    return lax.ppermute(x, "depth", route)


def swap_cores(x):
    return lax.ppermute(x, "depth", [(i, i ^ 1) for i in range(lax.axis_size("depth"))])


def gather_chip(x):
    count = lax.axis_size("depth")
    groups = [[i, i + 1] for i in range(0, count, 2)]
    return lax.all_gather(x, "depth", axis_index_groups=groups)


def swap_tiles(x, first):
    route = []
    for i in range(first, lax.axis_size("tile") - 1, 2):
        route += [(i, i + 1), (i + 1, i)]
    return lax.ppermute(x, "tile", route)


def on_device(potential, probe, positions, intensity, fwd_wave, adj_wave, saved_wave):
    n = probe.shape[1]
    core, cols = potential.shape[1:]
    margin = (cols - core) // 2
    tall = core + 2 * margin + SUB
    spots = positions[0].T
    step_cost = pl.CostEstimate(flops=8 * 2 * n * n * n * 2, bytes_accessed=1 << 20, transcendentals=0)
    pair_cost = pl.CostEstimate(flops=2 * 8 * 2 * n * n * n * 2, bytes_accessed=1 << 20, transcendentals=0)
    edge_cost = pl.CostEstimate(flops=1 << 33, bytes_accessed=1 << 20, transcendentals=0)
    far = [pltpu.VMEM((2, n, n), F32)]
    extent = shape(tall, cols)
    edge = shape(margin, cols, dtype=BF16)
    half = shape(2, n, n, dtype=BF16)

    tables, prop = jnp.asarray(dft_matrices(n)), jnp.asarray(propagator(n))
    inner, outer = call(edges_kernel, "edges", [edge, edge], (potential,), cost=edge_cost)
    outer = swap_tiles(outer, 0)
    inner = swap_tiles(inner, 1)
    corners, tr, ti = call(
        first_kernel, "first", [shape(4 * TICKS + 8, LANES, dtype=jnp.int32), extent, extent], (spots, potential),
        cost=step_cost,
    )
    packed = (tall - SUB) * 3 // 2
    tr, ti, shared = call(
        share_kernel, "share", [extent] * 2 + [shape(2 * (TICKS - 1) * n + packed, n, dtype=BF16)],
        (inner, outer, potential, saved_wave, tr, ti), {4: 0, 5: 1},
    )
    shared = swap_cores(shared)
    common = (corners, saved_wave, intensity, tables, prop, tr, ti)
    entry = (fwd_wave, adj_wave)

    b, acc = call(first_step_kernel, "step0", [half, extent], common + entry, cost=step_cost, scratch=far)
    b = swap_chips(b)
    args = (*common, shared, *entry, acc)
    a, acc, mate_acc, mate_tr, mate_ti = call(
        functools.partial(pair_kernel, 0, True), "steps01", [half] + [extent] * 4, args, {len(args) - 1: 1}, pair_cost, far
    )
    a = ring(a)

    def pair(tick, recv, acc, mate_acc):
        args = (*common, shared, recv, probe, mate_tr, mate_ti, acc, mate_acc)
        return call(
            functools.partial(pair_kernel, tick, False), f"steps{tick}{tick + 1}", [half, extent, extent], args,
            {len(args) - 2: 1, len(args) - 1: 2}, pair_cost, far,
        )

    b, acc, mate_acc = pair(1, b, acc, mate_acc)
    b = cross(b)
    a, acc, mate_acc = pair(2, a, acc, mate_acc)
    a = ring(a)
    args = (corners, intensity, tables, prop, mate_tr, mate_ti, shared, b, probe, mate_acc)
    b, mate_acc, mate_sum = call(
        last_step_kernel, "step3", [half, extent, shape(packed, n, dtype=BF16)], args, {len(args) - 1: 1}, step_cost, far
    )
    inner, outer, acc = call(sum_kernel, "sum", [edge, edge, extent], (gather_chip(mate_sum), acc), {1: 2})
    outer = swap_tiles(outer, 0)
    inner = swap_tiles(inner, 1)
    wave, adj = call(
        waves_kernel, "waves", [shape(1, 1, 2, n, n), shape(1, 1, 2, n, n, dtype=BF16)], (a, b, probe)
    )
    acc, wave, adj = lax.optimization_barrier((acc, wave, adj))
    (grad,) = call(fold_kernel, "fold", [shape(1, core, cols)], (acc, inner, outer))
    return wave, adj, grad


def solution(mesh):
    placed = (
        P("depth", "tile", None),
        P(),
        P("tile", None, None),
        P("tile", None, None, None),
        P("depth", "tile", None, None, None),
        P("depth", "tile", None, None, None),
        P("depth", "tile", None, None, None, None),
    )
    return jax.shard_map(
        on_device,
        mesh=mesh,
        in_specs=placed,
        out_specs=(
            P("depth", "tile", None, None, None),
            P("depth", "tile", None, None, None),
            P("depth", "tile", None),
        ),
        check_vma=False,
    )
```

```python
import functools
import math

import jax
import jax.numpy as jnp
import numpy as np
from jax import lax
from jax.experimental import pallas as pl
from jax.experimental.pallas import tpu as pltpu
from jax.sharding import PartitionSpec as P

TICKS = 4
SIGMA = 0.8
DEFOCUS = 6.0
LANES = 128
SUB = 8
F32 = jnp.float32
BF16 = jnp.bfloat16


def halves(n):
    return np.concatenate([np.arange(0, n, 2), np.arange(1, n, 2)])


def dft_matrices(n):
    idx = np.arange(n)
    angle = ((idx[:, None] * idx[None, :]) % n).astype(np.float32) * np.float32(2.0 * math.pi / n)
    scale = np.float32(1.0 / math.sqrt(n))
    cos_t = np.cos(angle) * scale
    sin_t = np.sin(angle) * scale
    both = []
    for odd in range(2):
        c, s = cos_t[: n // 2, odd::2], sin_t[: n // 2, odd::2]
        both.append(np.block([[c, -s], [s, c]]))
    order = (halves(n)[:, None] == idx[None, :]).astype(np.float32)
    return np.stack([*both, both[0].T, both[1].T, order]).astype(BF16)


def propagator(n):
    freq = np.where(np.arange(n) < n // 2, np.arange(n), np.arange(n) - n).astype(np.float32)[halves(n)]
    square = freq[:, None] * freq[:, None] + freq[None, :] * freq[None, :]
    phase = np.float32(-math.pi * DEFOCUS) * square / np.float32(n * n)
    return np.stack([np.cos(phase), np.sin(phase)]).astype(np.float32)


def sin_cos(x):
    mid = 1.2
    y = x - mid
    z = y * y
    s = y * (1.0 + z * (-1.0 / 6 + z * (1.0 / 120 + z * (-1.0 / 5040 + z * (1.0 / 362880)))))
    c = 1.0 + z * (-0.5 + z * (1.0 / 24 + z * (-1.0 / 720 + z * (1.0 / 40320 + z * (-1.0 / 3628800)))))
    cm, sm = math.cos(mid), math.sin(mid)
    return s * cm + c * sm, c * cm - s * sm


def turned(x, back, size, axis):
    own = lax.broadcasted_iota(jnp.int32, x.shape, axis)
    return pltpu.roll(x, lax.rem(size - back, size), axis), own < size - back


def cut(ref, row, col, n):
    base = pl.multiple_of(row // SUB * SUB, SUB)
    groups = n // SUB + 1
    pieces = []
    for j in range(n // LANES + 1):
        x = ref[pl.ds(base, n + SUB), j * LANES : (j + 1) * LANES].reshape(groups, SUB, LANES)
        x, near = turned(x, row - base, SUB, 1)
        x = jnp.where(near[1:], x[:-1], x[1:]).reshape(n, LANES)
        pieces.append(turned(x, col, LANES, 1))
    return jnp.concatenate(
        [jnp.where(here[1], here[0], after[0]) for here, after in zip(pieces[:-1], pieces[1:])], axis=1
    )


def place(ref, row, col, block):
    n = block.shape[0]
    base = pl.multiple_of(row // SUB * SUB, SUB)
    groups = n // SUB
    zero = jnp.zeros((n, LANES), F32)
    pieces = [
        pltpu.roll(block[:, j * LANES : (j + 1) * LANES], lax.rem(col, LANES), 1) for j in range(n // LANES)
    ]
    far = lax.broadcasted_iota(jnp.int32, (n, LANES), 1) >= col
    gap = jnp.zeros((1, SUB, LANES), F32)
    low = lax.broadcasted_iota(jnp.int32, (groups + 1, SUB, LANES), 1) >= row - base
    for j, (before, here) in enumerate(zip([zero] + pieces, pieces + [zero])):
        x = jnp.where(far, here, before).reshape(groups, SUB, LANES)
        x = pltpu.roll(x, row - base, 1)
        x = jnp.where(low, jnp.concatenate([x, gap], 0), jnp.concatenate([gap, x], 0))
        spot = (pl.ds(base, n + SUB), slice(j * LANES, (j + 1) * LANES))
        ref[spot] = ref[spot] + x.reshape(n + SUB, LANES)


def dot(a, b):
    return jnp.dot(a, b, preferred_element_type=F32)


def beside(a, b):
    return jnp.concatenate([a.astype(BF16), b.astype(BF16)], axis=1)


def above(a, b):
    return jnp.concatenate([a.astype(BF16), b.astype(BF16)], axis=0)


def forward(xr, xi, tables):
    h = xr.shape[0] // 2
    xr, xi = xr.astype(F32), xi.astype(F32)
    even = dot(beside(xr[:, :h] + xr[:, h:], xi[:, :h] + xi[:, h:]), tables[0])
    odd = dot(beside(xr[:, :h] - xr[:, h:], xi[:, :h] - xi[:, h:]), tables[1])
    even_sum, even_gap = even[:h] + even[h:], even[:h] - even[h:]
    odd_sum, odd_gap = odd[:h] + odd[h:], odd[:h] - odd[h:]
    rows = []
    for table, e, o in ((2, even_sum, odd_sum), (3, even_gap, odd_gap)):
        rows.append(dot(tables[table], above(beside(e[:, :h], o[:, :h]), beside(e[:, h:], o[:, h:]))))
    return jnp.concatenate([r[:h] for r in rows], 0), jnp.concatenate([r[h:] for r in rows], 0)


def inverse(fr, fi, tables):
    h = fr.shape[0] // 2
    even = dot(beside(fr[:, :h], fi[:, :h]), tables[2])
    odd = dot(beside(fr[:, h:], fi[:, h:]), tables[3])
    low, high = even + odd, even - odd
    rows = []
    for table, at in ((0, slice(0, h)), (1, slice(h, 2 * h))):
        both = above(beside(low[at, :h], high[at, :h]), beside(low[at, h:], high[at, h:]))
        rows.append(dot(tables[table], both))
    even, odd = rows
    low, high = even + odd, even - odd
    return jnp.concatenate([low[:h], high[:h]], 0), jnp.concatenate([low[h:], high[h:]], 0)


def adjoint(lr, li, tables, prop):
    br, bi = forward(lr, li, tables)
    return inverse(br * prop[0] + bi * prop[1], bi * prop[0] - br * prop[1], tables)


def odd_tile():
    return lax.rem(lax.axis_index("tile"), 2) == 1


def edges_kernel(pot, inner, outer):
    margin = inner.shape[0]
    core = pot.shape[1]
    low = pot[0, :margin].astype(BF16)
    high = pot[0, core - margin :].astype(BF16)
    inner[...] = jnp.where(odd_tile(), high, low)
    outer[...] = jnp.where(odd_tile(), low, high)


def transmit(v, tr, ti, rows):
    s, c = sin_cos(SIGMA * v)
    tr[rows] = c
    ti[rows] = s


def window_of(section, tick, forward):
    return jnp.where(forward, tick - section + 2 * lax.axis_size("depth") - 1, tick + section)


def first_kernel(spots, pot, corners, tr, ti):
    core = pot.shape[1]
    margin = (tr.shape[0] - SUB - core) // 2
    section = lax.axis_index("depth")
    even = lax.rem(section, 2) == 0
    mate = jnp.where(even, section + 1, section - 1)
    which = lax.broadcasted_iota(jnp.int32, spots.shape, 1)
    windows = [window_of(section, 0, jnp.logical_not(even))]
    for tick in range(TICKS):
        windows += [window_of(section, tick, even), window_of(mate, tick, even)]
    windows[own(TICKS - 1)] = window_of(mate, TICKS - 1, jnp.logical_not(even))
    for i, mb in enumerate(windows):
        chosen = jnp.sum(jnp.where(which == mb, spots[...].astype(F32), 0.0), axis=1, keepdims=True)
        corners[2 * i : 2 * i + 2] = jnp.broadcast_to(chosen.astype(jnp.int32), (2, LANES))
    transmit(pot[0], tr, ti, slice(margin, margin + core))


def corner(corners, which):
    numbers = corners[...]
    return numbers[2 * which, 0], numbers[2 * which + 1, 0]


def own(tick):
    return 1 + 2 * tick


def mates(tick):
    return 2 + 2 * tick


def pack(ref, at, block):
    rows, n = block.shape[0], ref.shape[1]
    block = block.astype(BF16)
    ref[at : at + rows] = block[:, :n]
    ref[at + rows : at + rows + rows // 2, : n // 2] = block[: rows // 2, n:]
    ref[at + rows : at + rows + rows // 2, n // 2 :] = block[rows // 2 :, n:]


def unpack(rows, packed):
    n = packed.shape[1]
    return (
        (slice(0, rows), slice(0, n), packed[:rows]),
        (slice(0, rows // 2), slice(n, n + n // 2), packed[rows:, : n // 2]),
        (slice(rows // 2, rows), slice(n, n + n // 2), packed[rows:, n // 2 :]),
    )


def share_kernel(inner, outer, saved, tr0, ti0, tr, ti, shared):
    margin = inner.shape[0]
    rows = tr.shape[0] - SUB
    core = rows - 2 * margin
    low = jnp.where(odd_tile(), outer[...], inner[...])
    high = jnp.where(odd_tile(), inner[...], outer[...])
    transmit(low.astype(F32), tr, ti, slice(0, margin))
    transmit(high.astype(F32), tr, ti, slice(margin + core, 2 * margin + core))
    n = shared.shape[1]
    for tick in range(1, TICKS):
        for part in range(2):
            at = (2 * (tick - 1) + part) * n
            shared[at : at + n] = saved[0, 0, tick, part]
    at = 2 * (TICKS - 1) * n
    pack(shared, at, tr[:rows])
    pack(shared, at + rows * 3 // 2, ti[:rows])


def forward_step(xr, xi, section, tick, spot, tr, ti, intens, tables, prop, far):
    n = far.shape[1]
    wr = cut(tr, *spot, n)
    wi = cut(ti, *spot, n)
    xr, xi = xr.astype(F32), xi.astype(F32)
    br, bi = forward(wr * xr - wi * xi, wr * xi + wi * xr, tables)
    far[0] = br * prop[0] - bi * prop[1]
    far[1] = br * prop[1] + bi * prop[0]

    @pl.when(section == lax.axis_size("depth") - 1)
    def _():
        rows = dot(tables[4], intens[0, tick]).astype(BF16)
        ordered = lax.dot_general(rows, tables[4], (((1,), (1,)), ((), ())), preferred_element_type=F32)
        fr, fi = far[0], far[1]
        excess = fr * fr + fi * fi - ordered
        far[0] = excess * fr
        far[1] = excess * fi

    sr, si = inverse(far[0], far[1], tables)
    return sr.astype(BF16), si.astype(BF16)


def backward_step(lr, li, saved, spot, tr, ti, acc):
    n = lr.shape[0]
    wr = cut(tr, *spot, n)
    wi = cut(ti, *spot, n)
    br = wr * lr + wi * li
    bi = wr * li - wi * lr
    place(acc, *spot, SIGMA * (bi * saved[0].astype(F32) - br * saved[1].astype(F32)))
    return br.astype(BF16), bi.astype(BF16)


def entering(recv, probe, section):
    at_start = section == 0
    return [jnp.where(at_start, probe[part], recv[part]) for part in range(2)]


def first_step_kernel(corners, saved, intens, tables, prop, tr, ti, fwd, adj, out, acc, far):
    section = lax.axis_index("depth")
    even = lax.rem(section, 2) == 0
    spot = corner(corners, 0)
    acc[...] = jnp.zeros(acc.shape, F32)

    @pl.when(jnp.logical_not(even))
    def _():
        x = fwd[0, 0, 0], fwd[0, 0, 1]
        out[0], out[1] = forward_step(*x, section, 0, spot, tr, ti, intens, tables, prop, far)

    @pl.when(even)
    def _():
        theirs = saved[0, 0, 0, 0], saved[0, 0, 0, 1]
        x = adjoint(adj[0, 0, 0], adj[0, 0, 1], tables, prop)
        out[0], out[1] = backward_step(*x, theirs, spot, tr, ti, acc)


def last_step_kernel(corners, intens, tables, prop, mate_tr, mate_ti, shared, recv, probe, acc0, out, acc, packed, far):
    tick = TICKS - 1
    section = lax.axis_index("depth")
    even = lax.rem(section, 2) == 0
    n = far.shape[1]
    spot = corner(corners, own(tick))

    @pl.when(jnp.logical_not(even))
    def _():
        x = entering(recv, probe, section - 1)
        x = forward_step(*x, section - 1, tick, spot, mate_tr, mate_ti, intens, tables, prop, far)
        out[0], out[1] = x

    @pl.when(even)
    def _():
        x = adjoint(recv[0], recv[1], tables, prop)
        at = 2 * (tick - 1) * n
        theirs = shared[at : at + n], shared[at + n : at + 2 * n]
        out[0], out[1] = backward_step(*x, theirs, spot, mate_tr, mate_ti, acc)

    pack(packed, 0, acc[: acc.shape[0] - SUB])


def pair_kernel(tick, fresh, corners, saved, intens, tables, prop, tr, ti, shared, *refs):
    if fresh:
        fwd, adj, _, out, acc, mate_acc, mate_tr, mate_ti, far = refs
    else:
        recv, probe, mate_tr, mate_ti, _, _, out, acc, mate_acc, far = refs
    section = lax.axis_index("depth")
    even = lax.rem(section, 2) == 0
    n = far.shape[1]
    spot, mate_spot = corner(corners, own(tick)), corner(corners, mates(tick + 1))
    if fresh:
        rows = mate_tr.shape[0] - SUB
        at = 2 * (TICKS - 1) * n
        for target in (mate_tr, mate_ti):
            for where_rows, where_columns, t in unpack(rows, shared[at : at + rows * 3 // 2]):
                target[where_rows, where_columns] = t.astype(F32)
            at += rows * 3 // 2
        mate_acc[...] = jnp.zeros(mate_acc.shape, F32)

    @pl.when(even)
    def _():
        x = (fwd[0, 0, 0], fwd[0, 0, 1]) if fresh else entering(recv, probe, section)
        x = forward_step(*x, section, tick, spot, tr, ti, intens, tables, prop, far)
        x = forward_step(*x, section + 1, tick + 1, mate_spot, mate_tr, mate_ti, intens, tables, prop, far)
        out[0], out[1] = x

    @pl.when(jnp.logical_not(even))
    def _():
        x = (adj[0, 0, 0], adj[0, 0, 1]) if fresh else (recv[0], recv[1])
        x = adjoint(*x, tables, prop)
        x = backward_step(*x, (saved[0, 0, tick, 0], saved[0, 0, tick, 1]), spot, tr, ti, acc)
        x = adjoint(*x, tables, prop)
        at = 2 * tick * n
        theirs = shared[at : at + n], shared[at + n : at + 2 * n]
        x = backward_step(*x, theirs, mate_spot, mate_tr, mate_ti, mate_acc)
        out[0], out[1] = x


def sum_kernel(gathered, acc0, inner, outer, acc):
    other = 1 - lax.rem(lax.axis_index("depth"), 2)
    rows = acc.shape[0] - SUB
    margin = inner.shape[0]
    for where_rows, where_columns, part in unpack(rows, gathered[other]):
        acc[where_rows, where_columns] += part.astype(F32)
    low = acc[:margin].astype(BF16)
    high = acc[rows - margin : rows].astype(BF16)
    inner[...] = jnp.where(odd_tile(), high, low)
    outer[...] = jnp.where(odd_tile(), low, high)


def waves_kernel(swapped, stayed, probe, wave, adj):
    section = lax.axis_index("depth")
    even = lax.rem(section, 2) == 0

    @pl.when(even)
    def _():
        wave[0, 0] = jnp.where(section == 0, probe[...], swapped[...]).astype(F32)
        adj[0, 0] = stayed[...]

    @pl.when(jnp.logical_not(even))
    def _():
        wave[0, 0] = stayed[...].astype(F32)
        adj[0, 0] = swapped[...]


def fold_kernel(acc, inner, outer, grad):
    margin = inner.shape[0]
    core = grad.shape[1]
    from_low = jnp.where(odd_tile(), outer[...], inner[...])
    from_high = jnp.where(odd_tile(), inner[...], outer[...])
    grad[0, :margin] = acc[margin : 2 * margin] + from_low.astype(F32)
    grad[0, margin : core - margin] = acc[2 * margin : core]
    grad[0, core - margin :] = acc[core : core + margin] + from_high.astype(F32)


VM = pl.BlockSpec(memory_space=pltpu.VMEM)


def call(kernel, name, outs, args, aliases=None, cost=None, scratch=()):
    return pl.pallas_call(
        kernel,
        name=name,
        in_specs=[VM] * len(args),
        out_specs=[VM] * len(outs),
        out_shape=outs,
        scratch_shapes=scratch,
        input_output_aliases=aliases or {},
        compiler_params=pltpu.CompilerParams(vmem_limit_bytes=24 << 20),
        cost_estimate=cost,
    )(*args)


def shape(*dims, dtype=F32):
    return jax.ShapeDtypeStruct(dims, dtype)


def swap_chips(x):
    last = lax.axis_size("depth") - 1
    route = [(0, 0), (last, last)]
    for i in range(1, last, 2):
        route += [(i, i + 1), (i + 1, i)]
    return lax.ppermute(x, "depth", route)


def ring(x):
    last = lax.axis_size("depth") - 1
    route = [(last - 1, last), (1, 0)]
    for i in range(0, last - 1, 2):
        route += [(i, i + 2), (i + 3, i + 1)]
    return lax.ppermute(x, "depth", route)


def cross(x):
    last = lax.axis_size("depth") - 1
    route = [(last - 1, last - 1), (1, 1)]
    for i in range(0, last - 1, 2):
        route += [(i, i + 3), (i + 3, i)]
    return lax.ppermute(x, "depth", route)


def swap_cores(x):
    return lax.ppermute(x, "depth", [(i, i ^ 1) for i in range(lax.axis_size("depth"))])


def gather_chip(x):
    count = lax.axis_size("depth")
    groups = [[i, i + 1] for i in range(0, count, 2)]
    return lax.all_gather(x, "depth", axis_index_groups=groups)


def swap_tiles(x, first):
    route = []
    for i in range(first, lax.axis_size("tile") - 1, 2):
        route += [(i, i + 1), (i + 1, i)]
    return lax.ppermute(x, "tile", route)


def on_device(potential, probe, positions, intensity, fwd_wave, adj_wave, saved_wave):
    n = probe.shape[1]
    core, cols = potential.shape[1:]
    margin = (cols - core) // 2
    tall = core + 2 * margin + SUB
    spots = positions[0].T
    step_cost = pl.CostEstimate(flops=8 * 2 * n * n * n * 2, bytes_accessed=1 << 20, transcendentals=0)
    pair_cost = pl.CostEstimate(flops=2 * 8 * 2 * n * n * n * 2, bytes_accessed=1 << 20, transcendentals=0)
    edge_cost = pl.CostEstimate(flops=1 << 33, bytes_accessed=1 << 20, transcendentals=0)
    far = [pltpu.VMEM((2, n, n), F32)]
    extent = shape(tall, cols)
    edge = shape(margin, cols, dtype=BF16)
    half = shape(2, n, n, dtype=BF16)

    tables, prop = jnp.asarray(dft_matrices(n)), jnp.asarray(propagator(n))
    inner, outer = call(edges_kernel, "edges", [edge, edge], (potential,), cost=edge_cost)
    outer = swap_tiles(outer, 0)
    inner = swap_tiles(inner, 1)
    corners, tr, ti = call(
        first_kernel, "first", [shape(4 * TICKS + 8, LANES, dtype=jnp.int32), extent, extent], (spots, potential),
        cost=step_cost,
    )
    packed = (tall - SUB) * 3 // 2
    tr, ti, shared = call(
        share_kernel, "share", [extent] * 2 + [shape(2 * (TICKS - 1) * n + 2 * packed, n, dtype=BF16)],
        (inner, outer, saved_wave, tr, ti), {3: 0, 4: 1},
    )
    shared = swap_cores(shared)
    common = (corners, saved_wave, intensity, tables, prop, tr, ti)
    entry = (fwd_wave, adj_wave)

    b, acc = call(first_step_kernel, "step0", [half, extent], common + entry, cost=step_cost, scratch=far)
    b = swap_chips(b)
    args = (*common, shared, *entry, acc)
    a, acc, mate_acc, mate_tr, mate_ti = call(
        functools.partial(pair_kernel, 0, True), "steps01", [half] + [extent] * 4, args, {len(args) - 1: 1}, pair_cost, far
    )
    a = ring(a)

    def pair(tick, recv, acc, mate_acc):
        args = (*common, shared, recv, probe, mate_tr, mate_ti, acc, mate_acc)
        return call(
            functools.partial(pair_kernel, tick, False), f"steps{tick}{tick + 1}", [half, extent, extent], args,
            {len(args) - 2: 1, len(args) - 1: 2}, pair_cost, far,
        )

    b, acc, mate_acc = pair(1, b, acc, mate_acc)
    b = cross(b)
    a, acc, mate_acc = pair(2, a, acc, mate_acc)
    a = ring(a)
    args = (corners, intensity, tables, prop, mate_tr, mate_ti, shared, b, probe, mate_acc)
    b, mate_acc, mate_sum = call(
        last_step_kernel, "step3", [half, extent, shape(packed, n, dtype=BF16)], args, {len(args) - 1: 1}, step_cost, far
    )
    inner, outer, acc = call(sum_kernel, "sum", [edge, edge, extent], (gather_chip(mate_sum), acc), {1: 2})
    outer = swap_tiles(outer, 0)
    inner = swap_tiles(inner, 1)
    wave, adj = call(
        waves_kernel, "waves", [shape(1, 1, 2, n, n), shape(1, 1, 2, n, n, dtype=BF16)], (a, b, probe)
    )
    acc, wave, adj = lax.optimization_barrier((acc, wave, adj))
    (grad,) = call(fold_kernel, "fold", [shape(1, core, cols)], (acc, inner, outer))
    return wave, adj, grad


def solution(mesh):
    placed = (
        P("depth", "tile", None),
        P(),
        P("tile", None, None),
        P("tile", None, None, None),
        P("depth", "tile", None, None, None),
        P("depth", "tile", None, None, None),
        P("depth", "tile", None, None, None, None),
    )
    return jax.shard_map(
        on_device,
        mesh=mesh,
        in_specs=placed,
        out_specs=(
            P("depth", "tile", None, None, None),
            P("depth", "tile", None, None, None),
            P("depth", "tile", None),
        ),
        check_vma=False,
    )
```
